256 devices in a mesh: dp: 32 (over y_hi, z, core), proto: 8 (over y_lo, x).
Axes of the slice: x: 4, y: 4 (y_hi: 2, y_lo: 2; y = y_hi * 2 + y_lo), z: 8, core: 2. Of those that a mesh axis runs over, the one named last changes fastest.
Arguments:
- cls_features: bfloat16 [128, 384], P('dp')
- patch_features: bfloat16 [128, 256, 384], P('dp')
- mask_index: int32 [128, 64], P('dp'), may hold values from 0 to 255, as said below
- cls_protos: bfloat16 [384, 131072], P(None, ('proto', 'dp'))
- patch_protos: bfloat16 [384, 131072], P(None, ('proto', 'dp'))
Outputs:
- cls_targets: bfloat16 [128, 131072], P('dp', 'proto')
- patch_targets: bfloat16 [8192, 131072], P('dp', 'proto')
The draws below stay inside these ranges and needn't reach their ends.
Inputs may be any that keep to these rules, and one draw needn't show every extreme that they name: `mask_index`: the 64 numbers of one crop are distinct.
All inputs are finite; a program needn't handle non-finite values.
Results may differ from the reference program's by a relative error of at most 0.0036.
Values may be sent and summed in bfloat16 or wider, within the bound.
No kernel may reach another device: no remote copies, remote signals or barrier semaphores. Data moves between devices by JAX's collectives and lax.ppermute only.
A program may use at most 128 MiB of HBM per device.

```python
import jax
import jax.numpy as jnp
from jax import lax

PATCHES = 256
MASKED = 64
BOTTLE = 384
PROTOS = 131072
ITERS = 3
VIEWS = 128


def shared_direction(key):
    return jax.random.normal(key, (BOTTLE,), jnp.float32)


def leaning(key, direction, shape, low, high):
    strength = jax.random.uniform(jax.random.fold_in(key, 1), shape, jnp.float32, low, high)
    noise = jax.random.normal(jax.random.fold_in(key, 2), shape + (BOTTLE,), jnp.float32)
    return noise + strength[..., None] * direction


def draw_cls_features(key, part):
    direction = shared_direction(key)
    key = jax.random.fold_in(key, 3)
    values = leaning(key, direction, (VIEWS,), -2.0, 2.0)
    return values.astype(jnp.bfloat16)


def draw_patch_features(key, part):
    direction = shared_direction(key)
    key = jax.random.fold_in(key, 7)
    values = leaning(key, direction, (VIEWS, PATCHES), -2.0, 2.0)
    return values.astype(jnp.bfloat16)


def draw_cls_protos(key, part):
    direction = shared_direction(key)
    key = jax.random.fold_in(key, 5)
    values = leaning(key, direction, (PROTOS,), -2.0, 2.0)
    return jnp.transpose(values).astype(jnp.bfloat16)


def draw_patch_protos(key, part):
    direction = shared_direction(key)
    key = jax.random.fold_in(key, 9)
    values = leaning(key, direction, (PROTOS,), -2.0, 2.0)
    return jnp.transpose(values).astype(jnp.bfloat16)


def draw_mask_index(key, part):
    key = jax.random.fold_in(key, 11)
    keys = jax.random.split(key, VIEWS)
    picks = jax.vmap(lambda single: jax.random.permutation(single, PATCHES)[:MASKED])(keys)
    return picks.astype(jnp.int32)


def setup_inputs(seed: int = 0) -> dict:
    streams_of = jax.random.split(jax.random.key(seed), 6)
    return {
        "cls_features": draw_cls_features(jax.random.fold_in(streams_of[5], 71), 0),
        "patch_features": draw_patch_features(jax.random.fold_in(streams_of[5], 71), 0),
        "mask_index": draw_mask_index(jax.random.fold_in(streams_of[5], 71), 0),
        "cls_protos": draw_cls_protos(jax.random.fold_in(streams_of[5], 71), 0),
        "patch_protos": draw_patch_protos(jax.random.fold_in(streams_of[5], 71), 0),
    }


teacher_temp = 0.07

def unit_rows(values):
    wide = values.astype(jnp.float32)
    return (wide * lax.rsqrt(lax.optimization_barrier(jnp.sum(wide * wide, -1, keepdims=True)) + 1e-06)).astype(jnp.bfloat16)

def kernel_of(units, protos):
    wide = protos.astype(jnp.float32)
    colsq = lax.optimization_barrier(jnp.sum(wide * wide, 0))
    cosine = jnp.dot(units, protos, preferred_element_type=jnp.float32) * lax.rsqrt(colsq + 1e-06)
    return jnp.exp((cosine - 1.0) / teacher_temp)

def balance(kernel):
    row_scale = jnp.ones((kernel.shape[0],), jnp.float32)
    col_scale = jnp.ones((kernel.shape[1],), jnp.float32)
    for step in range(ITERS):
        col_scale = 1.0 / jnp.dot(row_scale, kernel, precision=lax.Precision.HIGHEST)
        row_scale = 1.0 / jnp.dot(kernel, col_scale, precision=lax.Precision.HIGHEST)
    return (PROTOS * row_scale[:, None] * kernel * col_scale[None, :]).astype(jnp.bfloat16)

def reference(cls_features, patch_features, mask_index, cls_protos, patch_protos):
    selected = jnp.take_along_axis(patch_features, mask_index[:, :, None], axis=1).reshape(-1, BOTTLE)
    cls_targets = balance(kernel_of(unit_rows(cls_features), cls_protos))
    patch_targets = balance(kernel_of(unit_rows(selected), patch_protos))
    return (cls_targets, patch_targets)
```

```python
import functools

import jax
import jax.numpy as jnp
import numpy as np
from jax import lax
from jax.experimental import pallas as pl
from jax.experimental.pallas import tpu as pltpu
from jax.sharding import PartitionSpec as P

PROTOS = 131072
ITERS = 3
TEMP = 0.07
SLOPE = float(1.0 / (TEMP * np.log(2.0)))
F32 = jnp.float32
BF16 = jnp.bfloat16
BOTH = ("dp", "proto")
MIB = 1 << 20

NZ, NX = 8, 4


def coords(g):
    d, p = g // 8, g % 8
    return d % 2, (d // 2) % NZ, d // (2 * NZ), p % NX, p // NX


def flat(core, z, yh, x, yl):
    return ((yh * NZ + z) * 2 + core) * 8 + yl * NX + x


def swap(dcore=0, dyh=0, dyl=0):
    pairs = []
    for g in range(256):
        core, z, yh, x, yl = coords(g)
        pairs.append((g, flat(core ^ dcore, z, yh ^ dyh, x, yl ^ dyl)))
    return pairs


def groups(key):
    found = {}
    for g in range(256):
        found.setdefault(key(*coords(g)), []).append(g)
    return [found[k] for k in sorted(found)]


CORE = swap(dcore=1)
Y_STEPS = ((1, 1), (1, 0), (0, 1))
GROUPS_Z = groups(lambda core, z, yh, x, yl: (core, yh, x, yl))
GROUPS_ZX = groups(lambda core, z, yh, x, yl: (core, yh, yl))


def exchange(value, group):
    return lax.all_to_all(value, BOTH, 0, 0, axis_index_groups=group, tiled=True)


VM = pl.BlockSpec(memory_space=pltpu.VMEM)
SM = pl.BlockSpec(memory_space=pltpu.SMEM)


def call(body, out_shape, n_in, name, scratch=(), smem_first=False, limit=24):
    specs = [VM] * n_in
    if smem_first:
        specs[0] = SM
    return pl.pallas_call(
        body,
        out_shape=out_shape,
        in_specs=specs,
        out_specs=jax.tree.map(lambda _: VM, out_shape),
        scratch_shapes=list(scratch),
        compiler_params=pltpu.CompilerParams(vmem_limit_bytes=limit * MIB),
        name=name,
    )


def shape(dims, dtype=F32):
    return jax.ShapeDtypeStruct(dims, dtype)


def down(row):
    return jnp.transpose(jnp.broadcast_to(row, (128, 128)))


def across(block):
    return jnp.sum(jnp.transpose(block), axis=0, keepdims=True)


def swapped(rows, step):
    return jnp.concatenate([rows[k ^ step : (k ^ step) + 1] for k in range(8)], axis=0)


def inv_norms(protos):
    wide = protos.astype(F32)
    return SLOPE * lax.rsqrt(jnp.sum(wide * wide, axis=0, keepdims=True) + 1e-06)


def unit(values):
    return (values * lax.rsqrt(jnp.sum(values * values, -1, keepdims=True) + 1e-06)).astype(BF16)


def units_body(where_ref, feat_ref, mask_ref, cls_ref, unit_ref, send_ref):
    for image in range(4):
        pick = lax.broadcasted_iota(jnp.int32, (256, 64), 0) == mask_ref[image : image + 1, :]
        chosen = lax.dot_general(
            pick.astype(BF16), feat_ref[image], (((0,), (0,)), ((), ())), preferred_element_type=F32
        )
        unit_ref[image * 64 : image * 64 + 64, :] = unit(chosen)
    half = unit_ref[pl.ds(pl.multiple_of(where_ref[4] * 128, 128), 128), :]
    cls = unit(cls_ref[...].astype(F32))
    tail = jnp.concatenate([cls.astype(F32), jnp.zeros((12, 384), F32)], axis=0).astype(BF16)
    for z in range(NZ):
        send_ref[z, :128, :] = half
        send_ref[z, 128:, :] = tail


def kernel_body(units_ref, *refs):
    pieces, (kern_ref, sums_ref) = refs[:8], refs[8:]
    for k in range(8):
        protos = pieces[k][...]
        scale = inv_norms(protos)

        def block(z, total):
            rows = pl.ds(pl.multiple_of(z * 128, 128), 128)
            dots = jnp.dot(units_ref[z, :128, :], protos, preferred_element_type=F32)
            value = jnp.exp2(dots * scale - SLOPE)
            kern_ref[rows, k * 512 : k * 512 + 512] = value
            return total + jnp.sum(value.reshape(16, 8, 512), axis=0)

        total = lax.fori_loop(0, NZ, block, jnp.zeros((8, 512), F32), unroll=2)
        sums_ref[k : k + 1, :] = jnp.sum(total, axis=0, keepdims=True)


def cls_step(cls_kern, row_scale):
    wide = down(row_scale)
    cols = [
        1.0 / jnp.sum(cls_kern[:, q * 128 : q * 128 + 128] * wide, axis=0, keepdims=True)
        for q in range(4)
    ]
    total = cls_kern[:, :128] * cols[0]
    for q in range(1, 4):
        total = total + cls_kern[:, q * 128 : q * 128 + 128] * cols[q]
    return cols, across(total)


def cls_body(units_ref, protos_ref, sums_ref, kern_ref, message_ref):
    protos = protos_ref[...]
    dots = jnp.dot(units_ref[...], protos, preferred_element_type=F32)
    kern_ref[...] = jnp.exp2(dots * inv_norms(protos) - SLOPE)
    _, sums = cls_step(kern_ref[...], jnp.ones((1, 128), F32))
    message_ref[:, :512] = sums_ref[...]
    message_ref[:, 512:] = jnp.broadcast_to(sums, (8, 128))


def columns_body(last, got_ref, kern_ref, cls_kern_ref, message_ref, *more):
    total = got_ref[0]
    for k in range(1, 32):
        total = total + got_ref[k]
    row_scale = 1.0 / total[:9]
    cls_kern = cls_kern_ref[...]
    cols, sums = cls_step(cls_kern, row_scale[8:9])
    if last:
        for q in range(4):
            more[0][:, q * 128 : q * 128 + 128] = cls_kern[:, q * 128 : q * 128 + 128] * cols[q]
    acc = more[-1]
    for z in range(NZ):
        wide = down(row_scale[z : z + 1]).reshape(16, 8, 128)
        for t in range(32):
            block = kern_ref[z * 128 : z * 128 + 128, t * 128 : t * 128 + 128]
            part = jnp.sum(block.reshape(16, 8, 128) * wide, axis=0)
            if z == 0:
                acc[:, t * 128 : t * 128 + 128] = part
            else:
                acc[:, t * 128 : t * 128 + 128] += part
    for k in range(8):
        message_ref[k : k + 1, :512] = jnp.sum(acc[:, k * 512 : k * 512 + 512], axis=0, keepdims=True)
    message_ref[:, 512:] = jnp.broadcast_to(sums, (8, 128))


def add_body(mine_ref, other_ref, out_ref):
    out_ref[...] = mine_ref[...] + swapped(other_ref[...], 4)


def rows_body(last, mine_ref, a_ref, b_ref, c_ref, kern_ref, send_ref, wide_ref):
    total = mine_ref[...]
    for ref, (dyh, dyl) in zip((a_ref, b_ref, c_ref), Y_STEPS):
        total = total + swapped(ref[...], dyh * 2 + dyl)
    cols = 1.0 / total[:, :512]
    cls = total[:1, 512:]
    for k in range(8):
        wide_ref[:, k * 512 : k * 512 + 512] = jnp.broadcast_to(cols[k : k + 1], (8, 512))
    sums = []
    for z in range(NZ):
        acc = jnp.zeros((16, 8, 128), F32)
        for t in range(32):
            block = kern_ref[z * 128 : z * 128 + 128, t * 128 : t * 128 + 128]
            acc = acc + block.reshape(16, 8, 128) * wide_ref[:, t * 128 : t * 128 + 128][None]
        sums.append(across(acc.reshape(128, 128)))
    if last:
        own = [cols[k : k + 1, q * 128 : q * 128 + 128] for k in (0, 2, 4, 6) for q in range(4)]
        own = jnp.concatenate(own, axis=0)
        rest = jnp.zeros((6, 128), F32)
        for z in range(NZ):
            block = jnp.concatenate([own, sums[z], cls, rest], axis=0)
            for x in range(NX):
                send_ref[z * NX + x] = block
    else:
        block = jnp.concatenate(sums + [cls, jnp.zeros((7, 128), F32)], axis=0)
        for k in range(32):
            send_ref[k] = block


def settle_body(where_ref, got_ref, cols_ref, sums_ref):
    core, yh, x = where_ref[0], where_ref[2], where_ref[3]
    for z in range(NZ):
        for cr in range(2):
            for yr in range(2):
                row = (jnp.bitwise_xor(yh, yr) * NZ + z) * 2 + jnp.bitwise_xor(core, cr)
                for q in range(4):
                    at = (cr * 2 + yr) * 4 + q
                    cols_ref[row, :, q * 128 : q * 128 + 128] = got_ref[z * NX + x, at : at + 1, :]
    total = got_ref[0, 16:24, :]
    for k in range(1, 32):
        total = total + got_ref[k, 16:24, :]
    sums_ref[...] = total


def final_body(where_ref, protos_ref, units_ref, cols_ref, mine_ref, other_ref, out_ref, wide_ref):
    step = pl.program_id(0)

    @pl.when(step == 0)
    def _():
        yl = where_ref[4]
        mine, other = mine_ref[:1], other_ref[:1]
        first = jnp.where(yl == 0, mine, other)
        second = jnp.where(yl == 0, other, mine)
        wide_ref[:128] = PROTOS / down(first)
        wide_ref[128:] = PROTOS / down(second)

    for piece in range(4):
        protos = protos_ref[:, piece * 512 : piece * 512 + 512]
        scale = inv_norms(protos)
        cols = cols_ref[step * 4 + piece]
        dots = jnp.dot(units_ref[...], protos, preferred_element_type=F32)
        value = jnp.exp2(dots * scale - SLOPE) * cols
        for q in range(4):
            out_ref[:, piece * 512 + q * 128 : piece * 512 + q * 128 + 128] = (
                value[:, q * 128 : q * 128 + 128] * wide_ref[...]
            ).astype(BF16)


def final(where, protos, units, cols, mine, other):
    width = 2048
    return pl.pallas_call(
        final_body,
        out_shape=shape((256, 16384), BF16),
        grid=(16384 // width,),
        in_specs=[
            SM,
            pl.BlockSpec((384, width), lambda i: (0, i)),
            VM,
            VM,
            VM,
            VM,
        ],
        out_specs=pl.BlockSpec((256, width), lambda i: (0, i)),
        scratch_shapes=[pltpu.VMEM((256, 128), F32)],
        compiler_params=pltpu.CompilerParams(vmem_limit_bytes=56 * MIB),
        name="final_scale",
    )(where, protos, units, cols, mine, other)


def per_device(cls_features, patch_features, mask_index, cls_protos, patch_protos):
    dp, proto = lax.axis_index("dp"), lax.axis_index("proto")
    core, z, yh = dp % 2, (dp // 2) % NZ, dp // (2 * NZ)
    x, yl = proto % NX, proto // NX
    where = jnp.stack([core, z, yh, x, yl]).astype(jnp.int32)

    gathered = lax.all_gather(patch_protos, "dp", axis=1, tiled=True)

    near = {(0, 0): patch_protos}
    for dyh, dyl in Y_STEPS:
        near[dyh, dyl] = lax.ppermute(patch_protos, BOTH, swap(dyh=dyh, dyl=dyl))
    pieces = [near[k // 2, k % 2] for k in range(4)]
    pieces += [lax.ppermute(piece, BOTH, CORE) for piece in pieces]

    units, send = call(
        units_body, (shape((256, 384), BF16), shape((NZ, 144, 384), BF16)), 4, "units", smem_first=True
    )(where, patch_features, mask_index, cls_features)
    rows = exchange(send, GROUPS_Z)

    kern, col_sums = call(
        kernel_body, (pltpu.VMEM((1024, 4096), F32), shape((8, 512))), 9, "patch_kernel"
    )(rows, *pieces)

    cls_units = rows[:, 128:132, :]
    other = lax.ppermute(cls_units, BOTH, CORE)
    cls_units = jnp.stack([jnp.where(core == 0, cls_units, other), jnp.where(core == 0, other, cls_units)], 1)
    other = lax.ppermute(cls_units, BOTH, swap(dyh=1))
    cls_units = jnp.stack([jnp.where(yh == 0, cls_units, other), jnp.where(yh == 0, other, cls_units)], 0)
    cls_kern, message = call(cls_body, (shape((128, 512)), shape((8, 640))), 3, "cls_kernel")(
        cls_units.reshape(128, 384), cls_protos, col_sums
    )

    for step in range(ITERS):
        last = step == ITERS - 1
        if step:
            outs = [shape((8, 640))]
            if last:
                outs.append(shape((128, 512)))
            done = call(
                functools.partial(columns_body, last), tuple(outs), 3, "column_sums", [pltpu.VMEM((8, 4096), F32)]
            )(got, kern, cls_kern)
            message = done[0]
        message = call(add_body, shape((8, 640)), 2, "add_core")(message, lax.ppermute(message, BOTH, CORE))
        parts = [lax.ppermute(message, BOTH, swap(dyh=dyh, dyl=dyl)) for dyh, dyl in Y_STEPS]
        send = call(
            functools.partial(rows_body, last),
            shape((32, 24 if last else 16, 128)),
            5,
            "row_sums",
            [pltpu.VMEM((8, 4096), F32)],
        )(message, *parts, kern)
        got = exchange(send, GROUPS_ZX)

    cols, sums = call(settle_body, (shape((32, 1, 512)), shape((8, 128))), 2, "settle", smem_first=True)(where, got)
    other = lax.ppermute(sums, BOTH, swap(dyl=1))
    patch_targets = final(where, gathered, units, cols, sums, other)

    cls_scaled = lax.all_to_all(done[1].reshape(32, 4, 512), "dp", 0, 0, tiled=True)
    cls_rows = PROTOS / lax.dynamic_slice(sums[1], (dp * 4,), (4,))
    cls_targets = (cls_scaled.transpose(1, 0, 2) * cls_rows[:, None, None]).astype(BF16).reshape(4, 16384)
    return (cls_targets, patch_targets)


def solution(mesh):
    return jax.shard_map(
        per_device,
        mesh=mesh,
        in_specs=(
            P("dp", None),
            P("dp", None, None),
            P("dp", None),
            P(None, ("proto", "dp")),
            P(None, ("proto", "dp")),
        ),
        out_specs=(P("dp", "proto"), P("dp", "proto")),
        check_vma=False,
    )
```

```python
import functools

import jax
import jax.numpy as jnp
import numpy as np
from jax import lax
from jax.experimental import pallas as pl
from jax.experimental.pallas import tpu as pltpu
from jax.sharding import PartitionSpec as P

PROTOS = 131072
ITERS = 3
TEMP = 0.07
SLOPE = float(1.0 / (TEMP * np.log(2.0)))
F32 = jnp.float32
BF16 = jnp.bfloat16
BOTH = ("dp", "proto")
MIB = 1 << 20

NZ, NX = 8, 4


def coords(g):
    d, p = g // 8, g % 8
    return d % 2, (d // 2) % NZ, d // (2 * NZ), p % NX, p // NX


def flat(core, z, yh, x, yl):
    return ((yh * NZ + z) * 2 + core) * 8 + yl * NX + x


def swap(dcore=0, dz=0, dyh=0, dx=0, dyl=0):
    pairs = []
    for g in range(256):
        core, z, yh, x, yl = coords(g)
        pairs.append((g, flat(core ^ dcore, z ^ dz, yh ^ dyh, x ^ dx, yl ^ dyl)))
    return pairs


def groups(key):
    found = {}
    for g in range(256):
        found.setdefault(key(*coords(g)), []).append(g)
    return [found[k] for k in sorted(found)]


CORE = swap(dcore=1)
Y_STEPS = ((1, 1), (1, 0), (0, 1))
GROUPS_Z = groups(lambda core, z, yh, x, yl: (core, yh, x, yl))
Z_FAR = swap(dz=4)
Z_NEAR = [swap(dz=k) for k in (3, 2, 1)]
X_STEPS = [swap(dx=k) for k in (2, 1, 3)]


def exchange(value, group):
    return lax.all_to_all(value, BOTH, 0, 0, axis_index_groups=group, tiled=True)


VM = pl.BlockSpec(memory_space=pltpu.VMEM)
SM = pl.BlockSpec(memory_space=pltpu.SMEM)


def call(body, out_shape, n_in, name, scratch=(), smem_first=False, limit=8):
    specs = [VM] * n_in
    if smem_first:
        specs[0] = SM
    return pl.pallas_call(
        body,
        out_shape=out_shape,
        in_specs=specs,
        out_specs=jax.tree.map(lambda _: VM, out_shape),
        scratch_shapes=list(scratch),
        compiler_params=pltpu.CompilerParams(vmem_limit_bytes=limit * MIB),
        name=name,
    )


def shape(dims, dtype=F32):
    return jax.ShapeDtypeStruct(dims, dtype)


def down(row):
    return jnp.transpose(jnp.broadcast_to(row, (128, 128)))


def across(block):
    return jnp.sum(jnp.transpose(block), axis=0, keepdims=True)


def swapped(rows, step):
    return jnp.concatenate([rows[k ^ step : (k ^ step) + 1] for k in range(8)], axis=0)


def inv_norms(protos):
    wide = protos.astype(F32)
    return SLOPE * lax.rsqrt(jnp.sum(wide * wide, axis=0, keepdims=True) + 1e-06)


def unit(values):
    return (values * lax.rsqrt(jnp.sum(values * values, -1, keepdims=True) + 1e-06)).astype(BF16)


def units_body(where_ref, feat_ref, mask_ref, cls_ref, unit_ref, send_ref):
    for image in range(4):
        pick = lax.broadcasted_iota(jnp.int32, (256, 64), 0) == mask_ref[image : image + 1, :]
        chosen = lax.dot_general(
            pick.astype(BF16), feat_ref[image], (((0,), (0,)), ((), ())), preferred_element_type=F32
        )
        unit_ref[image * 64 : image * 64 + 64, :] = unit(chosen)
    half = unit_ref[pl.ds(pl.multiple_of(where_ref[4] * 128, 128), 128), :]
    cls = unit(cls_ref[...].astype(F32))
    tail = jnp.concatenate([cls.astype(F32), jnp.zeros((12, 384), F32)], axis=0).astype(BF16)
    for z in range(NZ):
        send_ref[z, :128, :] = half
        send_ref[z, 128:, :] = tail


def kernel_body(units_ref, *refs):
    pieces, (kern_ref, sums_ref) = refs[:8], refs[8:]
    for k in range(8):
        for half in range(2):
            protos = pieces[k][:, half * 256 : half * 256 + 256]
            scale = inv_norms(protos)
            total = jnp.zeros((8, 256), F32)
            for part in range(2):
                units = units_ref[part * 4 : part * 4 + 4, :128, :].reshape(512, 384)
                dots = jnp.dot(units, protos, preferred_element_type=F32)
                value = jnp.exp2(dots * scale - SLOPE)
                at = k * 512 + half * 256
                kern_ref[part * 512 : part * 512 + 512, at : at + 256] = value
                total = total + jnp.sum(value.reshape(64, 8, 256), axis=0)
            sums_ref[k : k + 1, half * 256 : half * 256 + 256] = jnp.sum(total, axis=0, keepdims=True)


def cls_step(cls_kern, row_scale):
    wide = down(row_scale)
    cols = [
        1.0 / jnp.sum(cls_kern[:, q * 128 : q * 128 + 128] * wide, axis=0, keepdims=True)
        for q in range(4)
    ]
    total = cls_kern[:, :128] * cols[0]
    for q in range(1, 4):
        total = total + cls_kern[:, q * 128 : q * 128 + 128] * cols[q]
    return cols, across(total)


def cls_body(where_ref, mine_ref, other_ref, protos_ref, sums_ref, kern_ref, message_ref):
    core, yh = where_ref[0], where_ref[2]
    both = []
    for ref in (mine_ref, other_ref):
        near = jnp.concatenate([ref[0, z].astype(F32) for z in range(NZ)], axis=0)
        far = jnp.concatenate([ref[1, z].astype(F32) for z in range(NZ)], axis=0)
        both.append(jnp.concatenate([jnp.where(core == 0, near, far), jnp.where(core == 0, far, near)], axis=0))
    units = jnp.concatenate([jnp.where(yh == 0, both[0], both[1]), jnp.where(yh == 0, both[1], both[0])], axis=0)
    protos = protos_ref[...]
    dots = jnp.dot(units.astype(BF16), protos, preferred_element_type=F32)
    kern_ref[...] = jnp.exp2(dots * inv_norms(protos) - SLOPE)
    _, sums = cls_step(kern_ref[...], jnp.ones((1, 128), F32))
    message_ref[:, :512] = sums_ref[...]
    message_ref[:, 512:] = jnp.broadcast_to(sums, (8, 128))


def columns_body(last, mine_ref, a_ref, b_ref, c_ref, kern_ref, cls_kern_ref, message_ref, *more):
    row_scale = 1.0 / (mine_ref[:9] + a_ref[:9] + b_ref[:9] + c_ref[:9])
    cls_kern = cls_kern_ref[...]
    cols, sums = cls_step(cls_kern, row_scale[8:9])
    if last:
        for q in range(4):
            scaled = cls_kern[:, q * 128 : q * 128 + 128] * cols[q]
            for n in range(32):
                yh, core, z = n // 16, (n // 8) % 2, n % 8
                more[0][(yh * NZ + z) * 2 + core, :, q * 128 : q * 128 + 128] = scaled[n * 4 : n * 4 + 4]
    acc = more[-1]
    for z in range(NZ):
        wide = down(row_scale[z : z + 1]).reshape(16, 8, 128)
        for t in range(32):
            block = kern_ref[z * 128 : z * 128 + 128, t * 128 : t * 128 + 128]
            part = jnp.sum(block.reshape(16, 8, 128) * wide, axis=0)
            if z == 0:
                acc[:, t * 128 : t * 128 + 128] = part
            else:
                acc[:, t * 128 : t * 128 + 128] += part
    for k in range(8):
        message_ref[k : k + 1, :512] = jnp.sum(acc[:, k * 512 : k * 512 + 512], axis=0, keepdims=True)
    message_ref[:, 512:] = jnp.broadcast_to(sums, (8, 128))


def add_body(mine_ref, other_ref, out_ref):
    out_ref[...] = mine_ref[...] + swapped(other_ref[...], 4)


def rows_body(last, mine_ref, a_ref, b_ref, c_ref, kern_ref, send_ref, wide_ref):
    total = mine_ref[...]
    for ref, (dyh, dyl) in zip((a_ref, b_ref, c_ref), Y_STEPS):
        total = total + swapped(ref[...], dyh * 2 + dyl)
    cols = 1.0 / total[:, :512]
    cls = total[:1, 512:]
    for k in range(8):
        wide_ref[:, k * 512 : k * 512 + 512] = jnp.broadcast_to(cols[k : k + 1], (8, 512))
    sums = []
    for z in range(NZ):
        acc = jnp.zeros((16, 8, 128), F32)
        for t in range(32):
            block = kern_ref[z * 128 : z * 128 + 128, t * 128 : t * 128 + 128]
            acc = acc + block.reshape(16, 8, 128) * wide_ref[:, t * 128 : t * 128 + 128][None]
        sums.append(across(acc.reshape(128, 128)))
    parts = sums + [cls, jnp.zeros((7, 128), F32)]
    if last:
        parts += [cols[k : k + 1, q * 128 : q * 128 + 128] for k in (0, 2, 4, 6) for q in range(4)]
    send_ref[...] = jnp.concatenate(parts, axis=0)


def far_body(mine_ref, other_ref, out_ref):
    out_ref[:16] = mine_ref[:16] + other_ref[:16]
    out_ref[16:32] = mine_ref[16:]
    out_ref[32:] = other_ref[16:]


def settle_body(where_ref, mine_ref, a_ref, b_ref, c_ref, cols_ref, sums_ref):
    core, z, yh = where_ref[0], where_ref[1], where_ref[2]
    sums_ref[...] = mine_ref[:16] + a_ref[:16] + b_ref[:16] + c_ref[:16]
    for near, ref in zip((0, 3, 2, 1), (mine_ref, a_ref, b_ref, c_ref)):
        for far in range(2):
            at_z = jnp.bitwise_xor(z, far * 4 + near)
            for cr in range(2):
                for yr in range(2):
                    row = (jnp.bitwise_xor(yh, yr) * NZ + at_z) * 2 + jnp.bitwise_xor(core, cr)
                    for q in range(4):
                        at = 16 + far * 16 + (cr * 2 + yr) * 4 + q
                        cols_ref[row, :, q * 128 : q * 128 + 128] = ref[at : at + 1, :]


def cls_final_body(where_ref, scaled_ref, sums_ref, out_ref):
    base = ((where_ref[2] * 2 + where_ref[0]) * NZ + where_ref[1]) * 4
    scale = PROTOS / sums_ref[8:9, :]
    lane = lax.broadcasted_iota(jnp.int32, (1, 128), 1)
    rows = [jnp.sum(jnp.where(lane == base + v, scale, 0.0), axis=1, keepdims=True) for v in range(4)]
    scale = jnp.concatenate(rows, axis=0)
    for d in range(32):
        out_ref[:, d * 512 : d * 512 + 512] = (scaled_ref[d] * scale).astype(BF16)


def final_body(where_ref, protos_ref, units_ref, cols_ref, mine_ref, other_ref, out_ref, wide_ref):
    step = pl.program_id(0)

    @pl.when(step == 0)
    def _():
        yl = where_ref[4]
        row = lax.broadcasted_iota(jnp.int32, (8, 128), 0) == where_ref[1]
        mine = jnp.sum(jnp.where(row, mine_ref[:8], 0.0), axis=0, keepdims=True)
        other = jnp.sum(jnp.where(row, other_ref[:8], 0.0), axis=0, keepdims=True)
        first = jnp.where(yl == 0, mine, other)
        second = jnp.where(yl == 0, other, mine)
        wide_ref[:128] = PROTOS / down(first)
        wide_ref[128:] = PROTOS / down(second)

    for piece in range(4):
        protos = protos_ref[:, piece * 512 : piece * 512 + 512]
        scale = inv_norms(protos)
        cols = cols_ref[step * 4 + piece]
        dots = jnp.dot(units_ref[...], protos, preferred_element_type=F32)
        value = jnp.exp2(dots * scale - SLOPE) * cols
        for q in range(4):
            out_ref[:, piece * 512 + q * 128 : piece * 512 + q * 128 + 128] = (
                value[:, q * 128 : q * 128 + 128] * wide_ref[...]
            ).astype(BF16)


def final(where, protos, units, cols, mine, other):
    width = 2048
    return pl.pallas_call(
        final_body,
        out_shape=shape((256, 16384), BF16),
        grid=(16384 // width,),
        in_specs=[
            SM,
            pl.BlockSpec((384, width), lambda i: (0, i)),
            VM,
            VM,
            VM,
            VM,
        ],
        out_specs=pl.BlockSpec((256, width), lambda i: (0, i)),
        scratch_shapes=[pltpu.VMEM((256, 128), F32)],
        compiler_params=pltpu.CompilerParams(vmem_limit_bytes=56 * MIB),
        name="final_scale",
    )(where, protos, units, cols, mine, other)


def per_device(cls_features, patch_features, mask_index, cls_protos, patch_protos):
    dp, proto = lax.axis_index("dp"), lax.axis_index("proto")
    core, z, yh = dp % 2, (dp // 2) % NZ, dp // (2 * NZ)
    x, yl = proto % NX, proto // NX
    where = jnp.stack([core, z, yh, x, yl]).astype(jnp.int32)

    gathered = lax.all_gather(patch_protos, "dp", axis=1, tiled=True)

    near = {(0, 0): patch_protos}
    for dyh, dyl in Y_STEPS:
        near[dyh, dyl] = lax.ppermute(patch_protos, BOTH, swap(dyh=dyh, dyl=dyl))
    pieces = [near[k // 2, k % 2] for k in range(4)]
    pieces += [lax.ppermute(piece, BOTH, CORE) for piece in pieces]

    units, send = call(
        units_body, (shape((256, 384), BF16), shape((NZ, 144, 384), BF16)), 4, "units", smem_first=True
    )(where, patch_features, mask_index, cls_features)
    rows = exchange(send, GROUPS_Z)

    kern, col_sums = call(
        kernel_body, (pltpu.VMEM((1024, 4096), F32), shape((8, 512))), 9, "patch_kernel"
    )(rows, *pieces)

    near = rows[:, 128:132, :]
    near = jnp.stack([near, lax.ppermute(near, BOTH, CORE)])
    far = lax.ppermute(near, BOTH, swap(dyh=1))
    cls_kern, message = call(
        cls_body, (shape((128, 512)), shape((8, 640))), 5, "cls_kernel", smem_first=True
    )(where, near, far, cls_protos, col_sums)

    for step in range(ITERS):
        last = step == ITERS - 1
        if step:
            outs = [shape((8, 640))]
            if last:
                outs.append(shape((32, 4, 512)))
            done = call(
                functools.partial(columns_body, last), tuple(outs), 6, "column_sums", [pltpu.VMEM((8, 4096), F32)]
            )(sums, *parts, kern, cls_kern)
            message = done[0]
        message = call(add_body, shape((8, 640)), 2, "add_core")(message, lax.ppermute(message, BOTH, CORE))
        parts = [lax.ppermute(message, BOTH, swap(dyh=dyh, dyl=dyl)) for dyh, dyl in Y_STEPS]
        sums = call(
            functools.partial(rows_body, last),
            shape((32 if last else 16, 128)),
            5,
            "row_sums",
            [pltpu.VMEM((8, 4096), F32)],
        )(message, *parts, kern)
        if last:
            sums, cls_scaled = lax.optimization_barrier((sums, done[1]))
            cls_scaled = lax.all_to_all(cls_scaled, "dp", 0, 0, tiled=True)
            other = lax.ppermute(sums, BOTH, Z_FAR)
            sums = call(far_body, shape((48, 128)), 2, "add_far")(sums, other)
            parts = [lax.ppermute(sums, BOTH, near) for near in Z_NEAR]
            cols, sums = call(
                settle_body, (shape((32, 1, 512)), shape((16, 128))), 5, "settle", smem_first=True
            )(where, sums, *parts)
        else:
            sums = sums + lax.ppermute(sums, BOTH, Z_FAR)
            parts = [lax.ppermute(sums, BOTH, near) for near in Z_NEAR]
            sums = sums + parts[0] + parts[1] + parts[2]
        parts = [lax.ppermute(sums, BOTH, near) for near in X_STEPS]

    sums = sums + parts[0] + parts[1] + parts[2]
    other = lax.ppermute(sums, BOTH, swap(dyl=1))
    patch_targets = final(where, gathered, units, cols, sums, other)
    cls_targets = call(cls_final_body, shape((4, 16384), BF16), 3, "cls_final", smem_first=True)(
        where, cls_scaled, sums
    )
    return (cls_targets, patch_targets)


def solution(mesh):
    return jax.shard_map(
        per_device,
        mesh=mesh,
        in_specs=(
            P("dp", None),
            P("dp", None, None),
            P("dp", None),
            P(None, ("proto", "dp")),
            P(None, ("proto", "dp")),
        ),
        out_specs=(P("dp", "proto"), P("dp", "proto")),
        check_vma=False,
    )
```

```python
import functools

import jax
import jax.numpy as jnp
import numpy as np
from jax import lax
from jax.experimental import pallas as pl
from jax.experimental.pallas import tpu as pltpu
from jax.sharding import PartitionSpec as P

PROTOS = 131072
ITERS = 3
TEMP = 0.07
SLOPE = float(1.0 / (TEMP * np.log(2.0)))
F32 = jnp.float32
BF16 = jnp.bfloat16
BOTH = ("dp", "proto")
MIB = 1 << 20

NZ, NX = 8, 4


def coords(g):
    d, p = g // 8, g % 8
    return d % 2, (d // 2) % NZ, d // (2 * NZ), p % NX, p // NX


def flat(core, z, yh, x, yl):
    return ((yh * NZ + z) * 2 + core) * 8 + yl * NX + x


def swap(dcore=0, dz=0, dyh=0, dx=0, dyl=0):
    pairs = []
    for g in range(256):
        core, z, yh, x, yl = coords(g)
        pairs.append((g, flat(core ^ dcore, z ^ dz, yh ^ dyh, x ^ dx, yl ^ dyl)))
    return pairs


def groups(key):
    found = {}
    for g in range(256):
        found.setdefault(key(*coords(g)), []).append(g)
    return [found[k] for k in sorted(found)]


CORE = swap(dcore=1)
Y_STEPS = ((1, 1), (1, 0), (0, 1))
GROUPS_Z = groups(lambda core, z, yh, x, yl: (core, yh, x, yl))
Z_FAR = swap(dz=4)
Z_NEAR = [swap(dz=k) for k in (3, 2, 1)]
X_STEPS = [swap(dx=k) for k in (2, 1, 3)]


def exchange(value, group):
    return lax.all_to_all(value, BOTH, 0, 0, axis_index_groups=group, tiled=True)


VM = pl.BlockSpec(memory_space=pltpu.VMEM)
SM = pl.BlockSpec(memory_space=pltpu.SMEM)


def call(body, out_shape, n_in, name, scratch=(), smem_first=False, limit=8):
    specs = [VM] * n_in
    if smem_first:
        specs[0] = SM
    return pl.pallas_call(
        body,
        out_shape=out_shape,
        in_specs=specs,
        out_specs=jax.tree.map(lambda _: VM, out_shape),
        scratch_shapes=list(scratch),
        compiler_params=pltpu.CompilerParams(vmem_limit_bytes=limit * MIB),
        name=name,
    )


def shape(dims, dtype=F32):
    return jax.ShapeDtypeStruct(dims, dtype)


def down(row):
    return jnp.transpose(jnp.broadcast_to(row, (128, 128)))


def across(block):
    return jnp.sum(jnp.transpose(block), axis=0, keepdims=True)


def swapped(rows, step):
    return jnp.concatenate([rows[k ^ step : (k ^ step) + 1] for k in range(8)], axis=0)


def inv_norms(protos):
    wide = protos.astype(F32)
    return SLOPE * lax.rsqrt(jnp.sum(wide * wide, axis=0, keepdims=True) + 1e-06)


def unit(values):
    return (values * lax.rsqrt(jnp.sum(values * values, -1, keepdims=True) + 1e-06)).astype(BF16)


def units_body(where_ref, feat_ref, mask_ref, cls_ref, unit_ref, send_ref):
    for image in range(4):
        pick = lax.broadcasted_iota(jnp.int32, (256, 64), 0) == mask_ref[image : image + 1, :]
        chosen = lax.dot_general(
            pick.astype(BF16), feat_ref[image], (((0,), (0,)), ((), ())), preferred_element_type=F32
        )
        unit_ref[image * 64 : image * 64 + 64, :] = unit(chosen)
    half = unit_ref[pl.ds(pl.multiple_of(where_ref[4] * 128, 128), 128), :]
    cls = unit(cls_ref[...].astype(F32))
    tail = jnp.concatenate([cls.astype(F32), jnp.zeros((12, 384), F32)], axis=0).astype(BF16)
    for z in range(NZ):
        send_ref[z, :128, :] = half
        send_ref[z, 128:, :] = tail


def kernel_body(units_ref, *refs):
    pieces, (kern_ref, sums_ref) = refs[:8], refs[8:]
    for k in range(8):
        for half in range(2):
            protos = pieces[k][:, half * 256 : half * 256 + 256]
            scale = inv_norms(protos)
            total = jnp.zeros((8, 256), F32)
            for part in range(2):
                units = units_ref[part * 4 : part * 4 + 4, :128, :].reshape(512, 384)
                dots = jnp.dot(units, protos, preferred_element_type=F32)
                value = jnp.exp2(dots * scale - SLOPE)
                at = k * 512 + half * 256
                kern_ref[part * 512 : part * 512 + 512, at : at + 256] = value
                total = total + jnp.sum(value.reshape(64, 8, 256), axis=0)
            sums_ref[k : k + 1, half * 256 : half * 256 + 256] = jnp.sum(total, axis=0, keepdims=True)


def cls_step(cls_kern, row_scale):
    wide = down(row_scale)
    cols = [
        1.0 / jnp.sum(cls_kern[:, q * 128 : q * 128 + 128] * wide, axis=0, keepdims=True)
        for q in range(4)
    ]
    total = cls_kern[:, :128] * cols[0]
    for q in range(1, 4):
        total = total + cls_kern[:, q * 128 : q * 128 + 128] * cols[q]
    return cols, across(total)


def cls_body(where_ref, mine_ref, other_ref, protos_ref, sums_ref, kern_ref, message_ref):
    core, yh = where_ref[0], where_ref[2]
    both = []
    for ref in (mine_ref, other_ref):
        near = jnp.concatenate([ref[0, z].astype(F32) for z in range(NZ)], axis=0)
        far = jnp.concatenate([ref[1, z].astype(F32) for z in range(NZ)], axis=0)
        both.append(jnp.concatenate([jnp.where(core == 0, near, far), jnp.where(core == 0, far, near)], axis=0))
    units = jnp.concatenate([jnp.where(yh == 0, both[0], both[1]), jnp.where(yh == 0, both[1], both[0])], axis=0)
    protos = protos_ref[...]
    dots = jnp.dot(units.astype(BF16), protos, preferred_element_type=F32)
    kern_ref[...] = jnp.exp2(dots * inv_norms(protos) - SLOPE)
    _, sums = cls_step(kern_ref[...], jnp.ones((1, 128), F32))
    message_ref[:, :512] = sums_ref[...]
    message_ref[:, 512:] = jnp.broadcast_to(sums, (8, 128))


def columns_body(last, mine_ref, a_ref, b_ref, c_ref, kern_ref, cls_kern_ref, message_ref, *more):
    row_scale = 1.0 / (mine_ref[:9] + a_ref[:9] + b_ref[:9] + c_ref[:9])
    cls_kern = cls_kern_ref[...]
    cols, sums = cls_step(cls_kern, row_scale[8:9])
    if last:
        for q in range(4):
            scaled = cls_kern[:, q * 128 : q * 128 + 128] * cols[q]
            for n in range(32):
                yh, core, z = n // 16, (n // 8) % 2, n % 8
                more[0][(yh * NZ + z) * 2 + core, :, q * 128 : q * 128 + 128] = scaled[n * 4 : n * 4 + 4]
    acc = more[-1]
    for z in range(NZ):
        wide = down(row_scale[z : z + 1]).reshape(16, 8, 128)
        for t in range(32):
            block = kern_ref[z * 128 : z * 128 + 128, t * 128 : t * 128 + 128]
            part = jnp.sum(block.reshape(16, 8, 128) * wide, axis=0)
            if z == 0:
                acc[:, t * 128 : t * 128 + 128] = part
            else:
                acc[:, t * 128 : t * 128 + 128] += part
    for k in range(8):
        message_ref[k : k + 1, :512] = jnp.sum(acc[:, k * 512 : k * 512 + 512], axis=0, keepdims=True)
    message_ref[:, 512:] = jnp.broadcast_to(sums, (8, 128))


def add_body(mine_ref, other_ref, out_ref):
    out_ref[...] = mine_ref[...] + swapped(other_ref[...], 4)


def rows_body(last, mine_ref, a_ref, b_ref, c_ref, kern_ref, send_ref, wide_ref):
    total = mine_ref[...]
    for ref, (dyh, dyl) in zip((a_ref, b_ref, c_ref), Y_STEPS):
        total = total + swapped(ref[...], dyh * 2 + dyl)
    cols = 1.0 / total[:, :512]
    cls = total[:1, 512:]
    for k in range(8):
        wide_ref[:, k * 512 : k * 512 + 512] = jnp.broadcast_to(cols[k : k + 1], (8, 512))
    sums = []
    for z in range(NZ):
        acc = jnp.zeros((16, 8, 128), F32)
        for t in range(32):
            block = kern_ref[z * 128 : z * 128 + 128, t * 128 : t * 128 + 128]
            acc = acc + block.reshape(16, 8, 128) * wide_ref[:, t * 128 : t * 128 + 128][None]
        sums.append(across(acc.reshape(128, 128)))
    parts = sums + [cls, jnp.zeros((7, 128), F32)]
    if last:
        parts += [cols[k : k + 1, q * 128 : q * 128 + 128] for k in (0, 2, 4, 6) for q in range(4)]
    send_ref[...] = jnp.concatenate(parts, axis=0)


def far_body(mine_ref, other_ref, out_ref):
    out_ref[:16] = mine_ref[:16] + other_ref[:16]
    out_ref[16:32] = mine_ref[16:]
    out_ref[32:] = other_ref[16:]


def settle_body(where_ref, mine_ref, a_ref, b_ref, c_ref, cols_ref, sums_ref):
    core, z, yh = where_ref[0], where_ref[1], where_ref[2]
    sums_ref[...] = mine_ref[:16] + a_ref[:16] + b_ref[:16] + c_ref[:16]
    for near, ref in zip((0, 3, 2, 1), (mine_ref, a_ref, b_ref, c_ref)):
        for far in range(2):
            at_z = jnp.bitwise_xor(z, far * 4 + near)
            for cr in range(2):
                for yr in range(2):
                    row = (jnp.bitwise_xor(yh, yr) * NZ + at_z) * 2 + jnp.bitwise_xor(core, cr)
                    for q in range(4):
                        at = 16 + far * 16 + (cr * 2 + yr) * 4 + q
                        cols_ref[row, :, q * 128 : q * 128 + 128] = ref[at : at + 1, :]


def cls_final_body(where_ref, scaled_ref, sums_ref, out_ref):
    base = ((where_ref[2] * 2 + where_ref[0]) * NZ + where_ref[1]) * 4
    scale = PROTOS / sums_ref[8:9, :]
    lane = lax.broadcasted_iota(jnp.int32, (1, 128), 1)
    rows = [jnp.sum(jnp.where(lane == base + v, scale, 0.0), axis=1, keepdims=True) for v in range(4)]
    scale = jnp.concatenate(rows, axis=0)
    for d in range(32):
        out_ref[:, d * 512 : d * 512 + 512] = (scaled_ref[d] * scale).astype(BF16)


WIDTH = 2048


def final_body(
    where_ref, protos_ref, units_ref, cols_ref, mine_ref, other_ref, out_ref, wide_ref, in_ref, stage_ref, in_sems, out_sems
):
    parts = 16384 // WIDTH
    lanes = [slice(n * WIDTH, n * WIDTH + WIDTH) for n in range(parts)]
    ins = [pltpu.make_async_copy(protos_ref.at[:, lanes[n]], in_ref.at[n], in_sems.at[n]) for n in range(parts)]
    outs = [pltpu.make_async_copy(stage_ref.at[n], out_ref.at[:, lanes[n]], out_sems.at[n]) for n in range(parts)]
    for copy in ins:
        copy.start()
    yl = where_ref[4]
    row = lax.broadcasted_iota(jnp.int32, (8, 128), 0) == where_ref[1]
    mine = jnp.sum(jnp.where(row, mine_ref[:8], 0.0), axis=0, keepdims=True)
    other = jnp.sum(jnp.where(row, other_ref[:8], 0.0), axis=0, keepdims=True)
    wide_ref[:128] = PROTOS / down(jnp.where(yl == 0, mine, other))
    wide_ref[128:] = PROTOS / down(jnp.where(yl == 0, other, mine))
    for n in range(parts):
        ins[n].wait()
        for at in range(0, WIDTH, 256):
            protos = in_ref[n, :, at : at + 256]
            cols = cols_ref[n * (WIDTH // 512) + at // 512][:, at % 512 : at % 512 + 256]
            dots = jnp.dot(units_ref[...], protos, preferred_element_type=F32)
            value = jnp.exp2(dots * inv_norms(protos) - SLOPE) * cols
            for q in (0, 128):
                scaled = value[:, q : q + 128] * wide_ref[...]
                stage_ref[n, :, at + q : at + q + 128] = scaled.astype(BF16)
        outs[n].start()
    for copy in outs:
        copy.wait()


def final(where, protos, units, cols, mine, other):
    parts = 16384 // WIDTH
    return pl.pallas_call(
        final_body,
        out_shape=shape((256, 16384), BF16),
        in_specs=[SM, pl.BlockSpec(memory_space=pl.ANY), VM, VM, VM, VM],
        out_specs=pl.BlockSpec(memory_space=pl.ANY),
        scratch_shapes=[
            pltpu.VMEM((256, 128), F32),
            pltpu.VMEM((parts, 384, WIDTH), BF16),
            pltpu.VMEM((parts, 256, WIDTH), BF16),
            pltpu.SemaphoreType.DMA((parts,)),
            pltpu.SemaphoreType.DMA((parts,)),
        ],
        compiler_params=pltpu.CompilerParams(vmem_limit_bytes=56 * MIB),
        name="final_scale",
    )(where, protos, units, cols, mine, other)


def per_device(cls_features, patch_features, mask_index, cls_protos, patch_protos):
    dp, proto = lax.axis_index("dp"), lax.axis_index("proto")
    core, z, yh = dp % 2, (dp // 2) % NZ, dp // (2 * NZ)
    x, yl = proto % NX, proto // NX
    where = jnp.stack([core, z, yh, x, yl]).astype(jnp.int32)

    near = {(0, 0): patch_protos}
    for dyh, dyl in Y_STEPS:
        near[dyh, dyl] = lax.ppermute(patch_protos, BOTH, swap(dyh=dyh, dyl=dyl))
    pieces = [near[k // 2, k % 2] for k in range(4)]
    pieces += [lax.ppermute(piece, BOTH, CORE) for piece in pieces]

    units, send = call(
        units_body, (shape((256, 384), BF16), shape((NZ, 144, 384), BF16)), 4, "units", smem_first=True
    )(where, patch_features, mask_index, cls_features)
    rows = exchange(send, GROUPS_Z)

    ahead = lax.optimization_barrier((patch_protos, rows, near[1, 1]))[0]
    gathered = lax.all_gather(ahead, "dp", axis=1, tiled=True)

    kern, col_sums = call(
        kernel_body, (pltpu.VMEM((1024, 4096), F32), shape((8, 512))), 9, "patch_kernel"
    )(rows, *pieces)

    near = rows[:, 128:132, :]
    near = jnp.stack([near, lax.ppermute(near, BOTH, CORE)])
    far = lax.ppermute(near, BOTH, swap(dyh=1))
    cls_kern, message = call(
        cls_body, (shape((128, 512)), shape((8, 640))), 5, "cls_kernel", smem_first=True
    )(where, near, far, cls_protos, col_sums)

    for step in range(ITERS):
        last = step == ITERS - 1
        if step:
            outs = [shape((8, 640))]
            if last:
                outs.append(shape((32, 4, 512)))
            done = call(
                functools.partial(columns_body, last), tuple(outs), 6, "column_sums", [pltpu.VMEM((8, 4096), F32)]
            )(sums, *parts, kern, cls_kern)
            message = done[0]
        message = call(add_body, shape((8, 640)), 2, "add_core")(message, lax.ppermute(message, BOTH, CORE))
        parts = [lax.ppermute(message, BOTH, swap(dyh=dyh, dyl=dyl)) for dyh, dyl in Y_STEPS]
        sums = call(
            functools.partial(rows_body, last),
            shape((32 if last else 16, 128)),
            5,
            "row_sums",
            [pltpu.VMEM((8, 4096), F32)],
        )(message, *parts, kern)
        if last:
            other = lax.ppermute(sums, BOTH, Z_FAR)
            sums = call(far_body, shape((48, 128)), 2, "add_far")(sums, other)
            parts = [lax.ppermute(sums, BOTH, near) for near in Z_NEAR]
            cols, sums = call(
                settle_body, (shape((32, 1, 512)), shape((16, 128))), 5, "settle", smem_first=True
            )(where, sums, *parts)
            cls_scaled = lax.optimization_barrier((done[1], sums))[0]
            cls_scaled = lax.all_to_all(cls_scaled, "dp", 0, 0, tiled=True)
        else:
            sums = sums + lax.ppermute(sums, BOTH, Z_FAR)
            parts = [lax.ppermute(sums, BOTH, near) for near in Z_NEAR]
            sums = sums + parts[0] + parts[1] + parts[2]
        parts = [lax.ppermute(sums, BOTH, near) for near in X_STEPS]

    sums = sums + parts[0] + parts[1] + parts[2]
    other = lax.ppermute(sums, BOTH, swap(dyl=1))
    patch_targets = final(where, gathered, units, cols, sums, other)
    cls_targets = call(cls_final_body, shape((4, 16384), BF16), 3, "cls_final", smem_first=True)(
        where, cls_scaled, sums
    )
    return (cls_targets, patch_targets)


def solution(mesh):
    return jax.shard_map(
        per_device,
        mesh=mesh,
        in_specs=(
            P("dp", None),
            P("dp", None, None),
            P("dp", None),
            P(None, ("proto", "dp")),
            P(None, ("proto", "dp")),
        ),
        out_specs=(P("dp", "proto"), P("dp", "proto")),
        check_vma=False,
    )
```

```python
import functools

import jax
import jax.numpy as jnp
import numpy as np
from jax import lax
from jax.experimental import pallas as pl
from jax.experimental.pallas import tpu as pltpu
from jax.sharding import PartitionSpec as P

PROTOS = 131072
ITERS = 3
TEMP = 0.07
SLOPE = float(1.0 / (TEMP * np.log(2.0)))
F32 = jnp.float32
BF16 = jnp.bfloat16
BOTH = ("dp", "proto")
MIB = 1 << 20

NZ, NX = 8, 4


def coords(g):
    d, p = g // 8, g % 8
    return d % 2, (d // 2) % NZ, d // (2 * NZ), p % NX, p // NX


def flat(core, z, yh, x, yl):
    return ((yh * NZ + z) * 2 + core) * 8 + yl * NX + x


def swap(dcore=0, dz=0, dyh=0, dx=0, dyl=0):
    pairs = []
    for g in range(256):
        core, z, yh, x, yl = coords(g)
        pairs.append((g, flat(core ^ dcore, z ^ dz, yh ^ dyh, x ^ dx, yl ^ dyl)))
    return pairs


def groups(key):
    found = {}
    for g in range(256):
        found.setdefault(key(*coords(g)), []).append(g)
    return [found[k] for k in sorted(found)]


CORE = swap(dcore=1)
Y_STEPS = ((1, 1), (1, 0), (0, 1))
GROUPS_Z = groups(lambda core, z, yh, x, yl: (core, yh, x, yl))
GROUPS_ZX = groups(lambda core, z, yh, x, yl: (core, yh, yl))


def exchange(value, group):
    return lax.all_to_all(value, BOTH, 0, 0, axis_index_groups=group, tiled=True)


VM = pl.BlockSpec(memory_space=pltpu.VMEM)
SM = pl.BlockSpec(memory_space=pltpu.SMEM)
HBM = pl.BlockSpec(memory_space=pltpu.HBM)


def call(body, out_shape, specs, name, scratch=(), limit=8):
    return pl.pallas_call(
        body,
        out_shape=out_shape,
        in_specs=specs,
        out_specs=jax.tree.map(lambda _: VM, out_shape),
        scratch_shapes=list(scratch),
        compiler_params=pltpu.CompilerParams(vmem_limit_bytes=limit * MIB),
        name=name,
    )


def shape(dims, dtype=F32):
    return jax.ShapeDtypeStruct(dims, dtype)


def down(row):
    return jnp.transpose(jnp.broadcast_to(row, (128, 128)))


def across(block):
    return jnp.sum(jnp.transpose(block), axis=0, keepdims=True)


def swapped(rows, step):
    return jnp.concatenate([rows[k ^ step : (k ^ step) + 1] for k in range(8)], axis=0)


def inv_norms(protos):
    wide = protos.astype(F32)
    return SLOPE * lax.rsqrt(jnp.sum(wide * wide, axis=0, keepdims=True) + 1e-06)


def unit(values):
    return (values * lax.rsqrt(jnp.sum(values * values, -1, keepdims=True) + 1e-06)).astype(BF16)


def units_body(where_ref, feat_ref, mask_ref, cls_ref, a_ref, b_ref, c_ref, unit_ref, send_ref):
    core, yh = where_ref[0], where_ref[2]
    for image in range(4):
        pick = lax.broadcasted_iota(jnp.int32, (256, 64), 0) == mask_ref[image : image + 1, :]
        chosen = lax.dot_general(
            pick.astype(BF16), feat_ref[image], (((0,), (0,)), ((), ())), preferred_element_type=F32
        )
        unit_ref[image * 64 : image * 64 + 64, :] = unit(chosen)
    half = unit_ref[pl.ds(pl.multiple_of(where_ref[4] * 128, 128), 128), :]
    cls = [unit(ref[...].astype(F32)).astype(F32) for ref in (cls_ref, a_ref, b_ref, c_ref)]
    near = [jnp.where(core == 0, cls[0], cls[1]), jnp.where(core == 0, cls[1], cls[0])]
    far = [jnp.where(core == 0, cls[2], cls[3]), jnp.where(core == 0, cls[3], cls[2])]
    first = [jnp.where(yh == 0, n, f) for n, f in zip(near, far)]
    second = [jnp.where(yh == 0, f, n) for n, f in zip(near, far)]
    tail = jnp.concatenate(first + second, axis=0).astype(BF16)
    for z in range(NZ):
        send_ref[z, :128, :] = half
        send_ref[z, 128:, :] = tail


def kernel_body(units_ref, *refs):
    pieces, (kern_ref, sums_ref) = refs[:8], refs[8:]
    for k in range(8):
        for half in range(2):
            lanes = slice(half * 256, half * 256 + 256)
            protos = pieces[k][:, lanes]
            scale = inv_norms(protos)
            total = jnp.zeros((8, 256), F32)
            for part in range(2):
                units = units_ref[part * 4 : part * 4 + 4, :128, :].reshape(512, 384)
                dots = jnp.dot(units, protos, preferred_element_type=F32)
                value = jnp.exp2(dots * scale - SLOPE)
                at = k * 512 + half * 256
                kern_ref[part * 512 : part * 512 + 512, at : at + 256] = value
                total = total + jnp.sum(value.reshape(64, 8, 256), axis=0)
            sums_ref[k : k + 1, lanes] = jnp.sum(total, axis=0, keepdims=True)


def cls_step(cls_kern, row_scale):
    wide = down(row_scale)
    cols = [
        1.0 / jnp.sum(cls_kern[:, q * 128 : q * 128 + 128] * wide, axis=0, keepdims=True)
        for q in range(4)
    ]
    total = cls_kern[:, :128] * cols[0]
    for q in range(1, 4):
        total = total + cls_kern[:, q * 128 : q * 128 + 128] * cols[q]
    return cols, across(total)


def cls_body(units_ref, protos_ref, sums_ref, kern_ref, message_ref):
    units = jnp.concatenate([units_ref[z, 128:, :] for z in range(NZ)], axis=0)
    protos = protos_ref[...]
    dots = jnp.dot(units, protos, preferred_element_type=F32)
    kern_ref[...] = jnp.exp2(dots * inv_norms(protos) - SLOPE)
    _, sums = cls_step(kern_ref[...], jnp.ones((1, 128), F32))
    message_ref[:, :512] = sums_ref[...]
    message_ref[:, 512:] = jnp.broadcast_to(sums, (8, 128))


def columns_body(last, got_ref, kern_ref, cls_kern_ref, message_ref, *more):
    total = got_ref[0]
    for k in range(1, 32):
        total = total + got_ref[k]
    row_scale = 1.0 / total[:9]
    cls_kern = cls_kern_ref[...]
    cols, sums = cls_step(cls_kern, row_scale[8:9])
    if last:
        for q in range(4):
            scaled = cls_kern[:, q * 128 : q * 128 + 128] * cols[q]
            for n in range(32):
                z, yh, core = n // 4, (n // 2) % 2, n % 2
                more[0][(yh * NZ + z) * 2 + core, :, q * 128 : q * 128 + 128] = scaled[n * 4 : n * 4 + 4]
    acc = more[-1]
    for z in range(NZ):
        wide = down(row_scale[z : z + 1]).reshape(16, 8, 128)
        for t in range(32):
            block = kern_ref[z * 128 : z * 128 + 128, t * 128 : t * 128 + 128]
            part = jnp.sum(block.reshape(16, 8, 128) * wide, axis=0)
            if z == 0:
                acc[:, t * 128 : t * 128 + 128] = part
            else:
                acc[:, t * 128 : t * 128 + 128] += part
    for k in range(8):
        message_ref[k : k + 1, :512] = jnp.sum(acc[:, k * 512 : k * 512 + 512], axis=0, keepdims=True)
    message_ref[:, 512:] = jnp.broadcast_to(sums, (8, 128))


def add_body(mine_ref, other_ref, out_ref):
    out_ref[...] = mine_ref[...] + swapped(other_ref[...], 4)


def rows_body(last, mine_ref, a_ref, b_ref, c_ref, kern_ref, send_ref, wide_ref):
    total = mine_ref[...]
    for ref, (dyh, dyl) in zip((a_ref, b_ref, c_ref), Y_STEPS):
        total = total + swapped(ref[...], dyh * 2 + dyl)
    cols = 1.0 / total[:, :512]
    cls = total[:1, 512:]
    for k in range(8):
        wide_ref[:, k * 512 : k * 512 + 512] = jnp.broadcast_to(cols[k : k + 1], (8, 512))
    sums = []
    for z in range(NZ):
        acc = jnp.zeros((16, 8, 128), F32)
        for t in range(32):
            block = kern_ref[z * 128 : z * 128 + 128, t * 128 : t * 128 + 128]
            acc = acc + block.reshape(16, 8, 128) * wide_ref[:, t * 128 : t * 128 + 128][None]
        sums.append(across(acc.reshape(128, 128)))
    if last:
        own = [cols[k : k + 1, q * 128 : q * 128 + 128] for k in (0, 2, 4, 6) for q in range(4)]
        own = jnp.concatenate(own, axis=0)
        rest = jnp.zeros((6, 128), F32)
        for z in range(NZ):
            block = jnp.concatenate([own, sums[z], cls, rest], axis=0)
            for x in range(NX):
                send_ref[z * NX + x] = block
    else:
        block = jnp.concatenate(sums + [cls, jnp.zeros((7, 128), F32)], axis=0)
        for k in range(32):
            send_ref[k] = block


def settle_body(where_ref, got_ref, cols_ref, sums_ref):
    core, yh, x = where_ref[0], where_ref[2], where_ref[3]
    total = got_ref[0, 16:24, :]
    for k in range(1, 32):
        total = total + got_ref[k, 16:24, :]
    sums_ref[...] = total
    for z in range(NZ):
        for cr in range(2):
            for yr in range(2):
                row = (jnp.bitwise_xor(yh, yr) * NZ + z) * 2 + jnp.bitwise_xor(core, cr)
                for q in range(4):
                    at = (cr * 2 + yr) * 4 + q
                    cols_ref[row, :, q * 128 : q * 128 + 128] = got_ref[z * NX + x, at : at + 1, :]


def cls_final_body(where_ref, scaled_ref, sums_ref, out_ref):
    base = ((where_ref[1] * 2 + where_ref[2]) * 2 + where_ref[0]) * 4
    scale = PROTOS / sums_ref[1:2, :]
    lane = lax.broadcasted_iota(jnp.int32, (1, 128), 1)
    rows = [jnp.sum(jnp.where(lane == base + v, scale, 0.0), axis=1, keepdims=True) for v in range(4)]
    scale = jnp.concatenate(rows, axis=0)
    for d in range(32):
        out_ref[:, d * 512 : d * 512 + 512] = (scaled_ref[d] * scale).astype(BF16)


WIDTH = 2048


def final_body(
    where_ref, protos_ref, units_ref, cols_ref, mine_ref, other_ref, out_ref, wide_ref, in_ref, stage_ref, in_sems, out_sems
):
    parts = 16384 // WIDTH
    lanes = [slice(n * WIDTH, n * WIDTH + WIDTH) for n in range(parts)]
    ins = [pltpu.make_async_copy(protos_ref.at[:, lanes[n]], in_ref.at[n], in_sems.at[n]) for n in range(parts)]
    outs = [pltpu.make_async_copy(stage_ref.at[n], out_ref.at[:, lanes[n]], out_sems.at[n]) for n in range(parts)]
    for copy in ins:
        copy.start()
    yl = where_ref[4]
    mine, other = mine_ref[:1], other_ref[:1]
    wide_ref[:128] = PROTOS / down(jnp.where(yl == 0, mine, other))
    wide_ref[128:] = PROTOS / down(jnp.where(yl == 0, other, mine))
    for n in range(parts):
        ins[n].wait()
        for at in range(0, WIDTH, 256):
            protos = in_ref[n, :, at : at + 256]
            cols = cols_ref[n * (WIDTH // 512) + at // 512][:, at % 512 : at % 512 + 256]
            dots = jnp.dot(units_ref[...], protos, preferred_element_type=F32)
            value = jnp.exp2(dots * inv_norms(protos) - SLOPE) * cols
            for q in (0, 128):
                scaled = value[:, q : q + 128] * wide_ref[...]
                stage_ref[n, :, at + q : at + q + 128] = scaled.astype(BF16)
        outs[n].start()
    for copy in outs:
        copy.wait()


def final(where, protos, units, cols, mine, other):
    parts = 16384 // WIDTH
    return pl.pallas_call(
        final_body,
        out_shape=shape((256, 16384), BF16),
        in_specs=[SM, HBM, VM, VM, VM, VM],
        out_specs=pl.BlockSpec(memory_space=pl.ANY),
        scratch_shapes=[
            pltpu.VMEM((256, 128), F32),
            pltpu.VMEM((parts, 384, WIDTH), BF16),
            pltpu.VMEM((parts, 256, WIDTH), BF16),
            pltpu.SemaphoreType.DMA((parts,)),
            pltpu.SemaphoreType.DMA((parts,)),
        ],
        compiler_params=pltpu.CompilerParams(vmem_limit_bytes=56 * MIB),
        name="final_scale",
    )(where, protos, units, cols, mine, other)


def per_device(cls_features, patch_features, mask_index, cls_protos, patch_protos):
    dp, proto = lax.axis_index("dp"), lax.axis_index("proto")
    core, z, yh = dp % 2, (dp // 2) % NZ, dp // (2 * NZ)
    x, yl = proto % NX, proto // NX
    where = jnp.stack([core, z, yh, x, yl]).astype(jnp.int32)

    gathered = lax.all_gather(patch_protos, "dp", axis=1, tiled=True)

    cls_near = [lax.ppermute(cls_features, BOTH, swap(dcore=c, dyh=h)) for c, h in ((1, 0), (0, 1), (1, 1))]

    near = {(0, 0): patch_protos}
    for dyh, dyl in Y_STEPS:
        near[dyh, dyl] = lax.ppermute(patch_protos, BOTH, swap(dyh=dyh, dyl=dyl))
    pieces = [near[k // 2, k % 2] for k in range(4)]
    pieces += [lax.ppermute(piece, BOTH, CORE) for piece in pieces]

    units, send = call(
        units_body, (shape((256, 384), BF16), shape((NZ, 144, 384), BF16)), [SM] + [VM] * 6, "units"
    )(where, patch_features, mask_index, cls_features, *cls_near)
    rows = exchange(send, GROUPS_Z)

    kern, col_sums = call(
        kernel_body, (pltpu.VMEM((1024, 4096), F32), shape((8, 512))), [VM] * 9, "patch_kernel"
    )(rows, *pieces)
    cls_kern, message = call(cls_body, (shape((128, 512)), shape((8, 640))), [VM] * 3, "cls_kernel")(
        rows, cls_protos, col_sums
    )

    for step in range(ITERS):
        last = step == ITERS - 1
        if step:
            outs = [shape((8, 640))]
            if last:
                outs.append(shape((32, 4, 512)))
            done = call(
                functools.partial(columns_body, last),
                tuple(outs),
                [VM] * 3,
                "column_sums",
                [pltpu.VMEM((8, 4096), F32)],
            )(got, kern, cls_kern)
            message = done[0]
        message = call(add_body, shape((8, 640)), [VM] * 2, "add_core")(message, lax.ppermute(message, BOTH, CORE))
        parts = [lax.ppermute(message, BOTH, swap(dyh=dyh, dyl=dyl)) for dyh, dyl in Y_STEPS]
        send = call(
            functools.partial(rows_body, last),
            shape((32, 24 if last else 16, 128)),
            [VM] * 5,
            "row_sums",
            [pltpu.VMEM((8, 4096), F32)],
        )(message, *parts, kern)
        got = exchange(send, GROUPS_ZX)

    cols, sums = call(settle_body, (shape((32, 1, 512)), shape((8, 128))), [SM, VM], "settle")(where, got)
    cls_scaled = lax.optimization_barrier((done[1], sums))[0]
    cls_scaled = lax.all_to_all(cls_scaled, "dp", 0, 0, tiled=True)
    other = lax.ppermute(sums, BOTH, swap(dyl=1))
    patch_targets = final(where, gathered, units, cols, sums, other)
    cls_scaled, patch_targets = lax.optimization_barrier((cls_scaled, patch_targets))
    cls_targets = call(cls_final_body, shape((4, 16384), BF16), [SM, VM, VM], "cls_final")(where, cls_scaled, sums)
    return (cls_targets, patch_targets)


def solution(mesh):
    return jax.shard_map(
        per_device,
        mesh=mesh,
        in_specs=(
            P("dp", None),
            P("dp", None, None),
            P("dp", None),
            P(None, ("proto", "dp")),
            P(None, ("proto", "dp")),
        ),
        out_specs=(P("dp", "proto"), P("dp", "proto")),
        check_vma=False,
    )
```

```python
import functools

import jax
import jax.numpy as jnp
import numpy as np
from jax import lax
from jax.experimental import pallas as pl
from jax.experimental.pallas import tpu as pltpu
from jax.sharding import PartitionSpec as P

PROTOS = 131072
ITERS = 3
TEMP = 0.07
SLOPE = float(1.0 / (TEMP * np.log(2.0)))
F32 = jnp.float32
BF16 = jnp.bfloat16
BOTH = ("dp", "proto")
MIB = 1 << 20

NZ, NX = 8, 4


def coords(g):
    d, p = g // 8, g % 8
    return d % 2, (d // 2) % NZ, d // (2 * NZ), p % NX, p // NX


def flat(core, z, yh, x, yl):
    return ((yh * NZ + z) * 2 + core) * 8 + yl * NX + x


def swap(dcore=0, dz=0, dyh=0, dx=0, dyl=0):
    pairs = []
    for g in range(256):
        core, z, yh, x, yl = coords(g)
        pairs.append((g, flat(core ^ dcore, z ^ dz, yh ^ dyh, x ^ dx, yl ^ dyl)))
    return pairs


def groups(key):
    found = {}
    for g in range(256):
        found.setdefault(key(*coords(g)), []).append(g)
    return [found[k] for k in sorted(found)]


CORE = swap(dcore=1)
Y_STEPS = ((1, 1), (1, 0), (0, 1))
GROUPS_Z = groups(lambda core, z, yh, x, yl: (core, yh, x, yl))
GROUPS_ZC = groups(lambda core, z, yh, x, yl: (yh, x, yl))
GROUPS_ZX = groups(lambda core, z, yh, x, yl: (core, yh, yl))


def exchange(value, group):
    return lax.all_to_all(value, BOTH, 0, 0, axis_index_groups=group, tiled=True)


VM = pl.BlockSpec(memory_space=pltpu.VMEM)
SM = pl.BlockSpec(memory_space=pltpu.SMEM)
HBM = pl.BlockSpec(memory_space=pltpu.HBM)


def call(body, out_shape, specs, name, scratch=(), limit=8):
    return pl.pallas_call(
        body,
        out_shape=out_shape,
        in_specs=specs,
        out_specs=jax.tree.map(lambda _: VM, out_shape),
        scratch_shapes=list(scratch),
        compiler_params=pltpu.CompilerParams(vmem_limit_bytes=limit * MIB),
        name=name,
    )


def shape(dims, dtype=F32):
    return jax.ShapeDtypeStruct(dims, dtype)


def down(row):
    return jnp.transpose(jnp.broadcast_to(row, (128, 128)))


def across(block):
    return jnp.sum(jnp.transpose(block), axis=0, keepdims=True)


def swapped(rows, step):
    return jnp.concatenate([rows[k ^ step : (k ^ step) + 1] for k in range(8)], axis=0)


def inv_norms(protos):
    wide = protos.astype(F32)
    return SLOPE * lax.rsqrt(jnp.sum(wide * wide, axis=0, keepdims=True) + 1e-06)


def unit(values):
    return (values * lax.rsqrt(jnp.sum(values * values, -1, keepdims=True) + 1e-06)).astype(BF16)


def units_body(where_ref, feat_ref, mask_ref, cls_ref, a_ref, b_ref, c_ref, unit_ref, send_ref):
    core, yh = where_ref[0], where_ref[2]
    for image in range(4):
        pick = lax.broadcasted_iota(jnp.int32, (256, 64), 0) == mask_ref[image : image + 1, :]
        chosen = lax.dot_general(
            pick.astype(BF16), feat_ref[image], (((0,), (0,)), ((), ())), preferred_element_type=F32
        )
        unit_ref[image * 64 : image * 64 + 64, :] = unit(chosen)
    half = unit_ref[pl.ds(pl.multiple_of(where_ref[4] * 128, 128), 128), :]
    cls = [unit(ref[...].astype(F32)).astype(F32) for ref in (cls_ref, a_ref, b_ref, c_ref)]
    near = [jnp.where(core == 0, cls[0], cls[1]), jnp.where(core == 0, cls[1], cls[0])]
    far = [jnp.where(core == 0, cls[2], cls[3]), jnp.where(core == 0, cls[3], cls[2])]
    first = [jnp.where(yh == 0, n, f) for n, f in zip(near, far)]
    second = [jnp.where(yh == 0, f, n) for n, f in zip(near, far)]
    tail = jnp.concatenate(first + second, axis=0).astype(BF16)
    for z in range(NZ):
        send_ref[z, :128, :] = half
        send_ref[z, 128:, :] = tail


def kernel_body(units_ref, *refs):
    pieces, (kern_ref, sums_ref) = refs[:8], refs[8:]
    for k in range(8):
        for half in range(2):
            lanes = slice(half * 256, half * 256 + 256)
            protos = pieces[k][:, lanes]
            scale = inv_norms(protos)
            total = jnp.zeros((8, 256), F32)
            for part in range(2):
                units = units_ref[part * 4 : part * 4 + 4, :128, :].reshape(512, 384)
                dots = jnp.dot(units, protos, preferred_element_type=F32)
                value = jnp.exp2(dots * scale - SLOPE)
                at = k * 512 + half * 256
                kern_ref[part * 512 : part * 512 + 512, at : at + 256] = value
                total = total + jnp.sum(value.reshape(64, 8, 256), axis=0)
            sums_ref[k : k + 1, lanes] = jnp.sum(total, axis=0, keepdims=True)


def cls_step(cls_kern, row_scale):
    wide = down(row_scale)
    cols = [
        1.0 / jnp.sum(cls_kern[:, q * 128 : q * 128 + 128] * wide, axis=0, keepdims=True)
        for q in range(4)
    ]
    total = cls_kern[:, :128] * cols[0]
    for q in range(1, 4):
        total = total + cls_kern[:, q * 128 : q * 128 + 128] * cols[q]
    return cols, across(total)


def cls_body(units_ref, protos_ref, sums_ref, kern_ref, message_ref):
    units = jnp.concatenate([units_ref[z, 128:, :] for z in range(NZ)], axis=0)
    protos = protos_ref[...]
    dots = jnp.dot(units, protos, preferred_element_type=F32)
    kern_ref[...] = jnp.exp2(dots * inv_norms(protos) - SLOPE)
    _, sums = cls_step(kern_ref[...], jnp.ones((1, 128), F32))
    message_ref[:, :512] = sums_ref[...]
    message_ref[:, 512:] = jnp.broadcast_to(sums, (8, 128))


def columns_body(last, got_ref, kern_ref, cls_kern_ref, message_ref, *more):
    total = got_ref[0]
    for k in range(1, 32):
        total = total + got_ref[k]
    row_scale = 1.0 / total[:9]
    cls_kern = cls_kern_ref[...]
    cols, sums = cls_step(cls_kern, row_scale[8:9])
    if last:
        for q in range(4):
            scaled = cls_kern[:, q * 128 : q * 128 + 128] * cols[q]
            for n in range(32):
                z, yh, core = n // 4, (n // 2) % 2, n % 2
                more[0][(yh * NZ + z) * 2 + core, :, q * 128 : q * 128 + 128] = scaled[n * 4 : n * 4 + 4]
    acc = more[-1]
    for z in range(NZ):
        wide = down(row_scale[z : z + 1]).reshape(16, 8, 128)
        for t in range(32):
            block = kern_ref[z * 128 : z * 128 + 128, t * 128 : t * 128 + 128]
            part = jnp.sum(block.reshape(16, 8, 128) * wide, axis=0)
            if z == 0:
                acc[:, t * 128 : t * 128 + 128] = part
            else:
                acc[:, t * 128 : t * 128 + 128] += part
    for k in range(8):
        message_ref[k : k + 1, :512] = jnp.sum(acc[:, k * 512 : k * 512 + 512], axis=0, keepdims=True)
    message_ref[:, 512:] = jnp.broadcast_to(sums, (8, 128))


def add_body(mine_ref, other_ref, out_ref):
    out_ref[...] = mine_ref[...] + swapped(other_ref[...], 4)


def rows_body(last, mine_ref, a_ref, b_ref, c_ref, kern_ref, send_ref, wide_ref):
    total = mine_ref[...]
    for ref, (dyh, dyl) in zip((a_ref, b_ref, c_ref), Y_STEPS):
        total = total + swapped(ref[...], dyh * 2 + dyl)
    cols = 1.0 / total[:, :512]
    cls = total[:1, 512:]
    for k in range(8):
        wide_ref[:, k * 512 : k * 512 + 512] = jnp.broadcast_to(cols[k : k + 1], (8, 512))
    sums = []
    for z in range(NZ):
        acc = jnp.zeros((16, 8, 128), F32)
        for t in range(32):
            block = kern_ref[z * 128 : z * 128 + 128, t * 128 : t * 128 + 128]
            acc = acc + block.reshape(16, 8, 128) * wide_ref[:, t * 128 : t * 128 + 128][None]
        sums.append(across(acc.reshape(128, 128)))
    if last:
        own = [cols[k : k + 1, q * 128 : q * 128 + 128] for k in (0, 2, 4, 6) for q in range(4)]
        own = jnp.concatenate(own, axis=0)
        rest = jnp.zeros((6, 128), F32)
        for z in range(NZ):
            block = jnp.concatenate([own, sums[z], cls, rest], axis=0)
            for x in range(NX):
                send_ref[z * NX + x] = block
    else:
        block = jnp.concatenate(sums + [cls, jnp.zeros((7, 128), F32)], axis=0)
        for k in range(32):
            send_ref[k] = block


def settle_body(where_ref, got_ref, cols_ref, sums_ref):
    core, yh, x = where_ref[0], where_ref[2], where_ref[3]
    total = got_ref[0, 16:24, :]
    for k in range(1, 32):
        total = total + got_ref[k, 16:24, :]
    sums_ref[...] = total
    for z in range(NZ):
        for cr in range(2):
            for yr in range(2):
                row = (jnp.bitwise_xor(yh, yr) * NZ + z) * 2 + jnp.bitwise_xor(core, cr)
                for q in range(4):
                    at = (cr * 2 + yr) * 4 + q
                    cols_ref[row, :, q * 128 : q * 128 + 128] = got_ref[z * NX + x, at : at + 1, :]


def cls_final_body(where_ref, scaled_ref, sums_ref, out_ref):
    base = ((where_ref[1] * 2 + where_ref[2]) * 2 + where_ref[0]) * 4
    scale = PROTOS / sums_ref[1:2, :]
    lane = lax.broadcasted_iota(jnp.int32, (1, 128), 1)
    rows = [jnp.sum(jnp.where(lane == base + v, scale, 0.0), axis=1, keepdims=True) for v in range(4)]
    scale = jnp.concatenate(rows, axis=0)
    for d in range(32):
        out_ref[:, d * 512 : d * 512 + 512] = (scaled_ref[d] * scale).astype(BF16)


PARTS = 8


def final_body(
    where_ref, near_ref, far_ref, units_ref, cols_ref, mine_ref, other_ref, out_ref, wide_ref, in_ref, stage_ref, in_sems, out_sems
):
    yh, yl = where_ref[2], where_ref[4]
    ins, outs, begins = [], [], []
    for n in range(PARTS):
        source = near_ref if n < PARTS // 2 else far_ref
        part = n % (PARTS // 2)
        begin = (yh if n < PARTS // 2 else 1 - yh) * 16 + part * 4
        lanes = pl.ds(pl.multiple_of(begin * 512, 2048), 2048)
        begins.append(begin)
        ins.append(pltpu.make_async_copy(source.at[pl.ds(part * 4, 4)], in_ref.at[n], in_sems.at[n]))
        outs.append(pltpu.make_async_copy(stage_ref.at[n], out_ref.at[:, lanes], out_sems.at[n]))
    for copy in ins:
        copy.start()
    mine, other = mine_ref[:1], other_ref[:1]
    wide_ref[:128] = PROTOS / down(jnp.where(yl == 0, mine, other))
    wide_ref[128:] = PROTOS / down(jnp.where(yl == 0, other, mine))
    for n in range(PARTS):
        ins[n].wait()
        for piece in range(4):
            for at in (0, 256):
                protos = in_ref[n, piece, :, at : at + 256]
                cols = cols_ref[begins[n] + piece][:, at : at + 256]
                dots = jnp.dot(units_ref[...], protos, preferred_element_type=F32)
                value = jnp.exp2(dots * inv_norms(protos) - SLOPE) * cols
                for q in (0, 128):
                    scaled = value[:, q : q + 128] * wide_ref[...]
                    to = piece * 512 + at + q
                    stage_ref[n, :, to : to + 128] = scaled.astype(BF16)
        outs[n].start()
    for copy in outs:
        copy.wait()


def final(where, near, far, units, cols, mine, other):
    return pl.pallas_call(
        final_body,
        out_shape=shape((256, 16384), BF16),
        in_specs=[SM, HBM, HBM, VM, VM, VM, VM],
        out_specs=pl.BlockSpec(memory_space=pl.ANY),
        scratch_shapes=[
            pltpu.VMEM((256, 128), F32),
            pltpu.VMEM((PARTS, 4, 384, 512), BF16),
            pltpu.VMEM((PARTS, 256, 2048), BF16),
            pltpu.SemaphoreType.DMA((PARTS,)),
            pltpu.SemaphoreType.DMA((PARTS,)),
        ],
        compiler_params=pltpu.CompilerParams(vmem_limit_bytes=56 * MIB),
        name="final_scale",
    )(where, near, far, units, cols, mine, other)


def per_device(cls_features, patch_features, mask_index, cls_protos, patch_protos):
    dp, proto = lax.axis_index("dp"), lax.axis_index("proto")
    core, z, yh = dp % 2, (dp // 2) % NZ, dp // (2 * NZ)
    x, yl = proto % NX, proto // NX
    where = jnp.stack([core, z, yh, x, yl]).astype(jnp.int32)

    cls_near = [lax.ppermute(cls_features, BOTH, swap(dcore=c, dyh=h)) for c, h in ((1, 0), (0, 1), (1, 1))]

    near = {(0, 0): patch_protos}
    for dyh, dyl in Y_STEPS:
        near[dyh, dyl] = lax.ppermute(patch_protos, BOTH, swap(dyh=dyh, dyl=dyl))
    pieces = [near[k // 2, k % 2] for k in range(4)]
    pieces += [lax.ppermute(piece, BOTH, CORE) for piece in pieces]

    units, send = call(
        units_body, (shape((256, 384), BF16), shape((NZ, 144, 384), BF16)), [SM] + [VM] * 6, "units"
    )(where, patch_features, mask_index, cls_features, *cls_near)
    rows = exchange(send, GROUPS_Z)

    held = lax.optimization_barrier((patch_protos, rows, *pieces[1:4]))[0]
    gathered = [lax.all_gather(held, BOTH, axis_index_groups=GROUPS_ZC)]
    gathered.append(lax.all_gather(near[1, 0], BOTH, axis_index_groups=GROUPS_ZC))

    kern, col_sums = call(
        kernel_body, (pltpu.VMEM((1024, 4096), F32), shape((8, 512))), [VM] * 9, "patch_kernel"
    )(rows, *pieces)
    cls_kern, message = call(cls_body, (shape((128, 512)), shape((8, 640))), [VM] * 3, "cls_kernel")(
        rows, cls_protos, col_sums
    )

    for step in range(ITERS):
        last = step == ITERS - 1
        if step:
            outs = [shape((8, 640))]
            if last:
                outs.append(shape((32, 4, 512)))
            done = call(
                functools.partial(columns_body, last),
                tuple(outs),
                [VM] * 3,
                "column_sums",
                [pltpu.VMEM((8, 4096), F32)],
            )(got, kern, cls_kern)
            message = done[0]
        message = call(add_body, shape((8, 640)), [VM] * 2, "add_core")(message, lax.ppermute(message, BOTH, CORE))
        parts = [lax.ppermute(message, BOTH, swap(dyh=dyh, dyl=dyl)) for dyh, dyl in Y_STEPS]
        send = call(
            functools.partial(rows_body, last),
            shape((32, 24 if last else 16, 128)),
            [VM] * 5,
            "row_sums",
            [pltpu.VMEM((8, 4096), F32)],
        )(message, *parts, kern)
        got = exchange(send, GROUPS_ZX)

    cols, sums = call(settle_body, (shape((32, 1, 512)), shape((8, 128))), [SM, VM], "settle")(where, got)
    cls_scaled = lax.optimization_barrier((done[1], sums))[0]
    cls_scaled = lax.all_to_all(cls_scaled, "dp", 0, 0, tiled=True)
    other = lax.ppermute(sums, BOTH, swap(dyl=1))
    patch_targets = final(where, *gathered, units, cols, sums, other)
    cls_scaled, patch_targets = lax.optimization_barrier((cls_scaled, patch_targets))
    cls_targets = call(cls_final_body, shape((4, 16384), BF16), [SM, VM, VM], "cls_final")(where, cls_scaled, sums)
    return (cls_targets, patch_targets)


def solution(mesh):
    return jax.shard_map(
        per_device,
        mesh=mesh,
        in_specs=(
            P("dp", None),
            P("dp", None, None),
            P("dp", None),
            P(None, ("proto", "dp")),
            P(None, ("proto", "dp")),
        ),
        out_specs=(P("dp", "proto"), P("dp", "proto")),
        check_vma=False,
    )
```

```python
import functools

import jax
import jax.numpy as jnp
import numpy as np
from jax import lax
from jax.experimental import pallas as pl
from jax.experimental.pallas import tpu as pltpu
from jax.sharding import PartitionSpec as P

PROTOS = 131072
ITERS = 3
TEMP = 0.07
SLOPE = float(1.0 / (TEMP * np.log(2.0)))
F32 = jnp.float32
BF16 = jnp.bfloat16
BOTH = ("dp", "proto")
MIB = 1 << 20

NZ, NX = 8, 4


def coords(g):
    d, p = g // 8, g % 8
    return d % 2, (d // 2) % NZ, d // (2 * NZ), p % NX, p // NX


def flat(core, z, yh, x, yl):
    return ((yh * NZ + z) * 2 + core) * 8 + yl * NX + x


def swap(dcore=0, dz=0, dyh=0, dx=0, dyl=0):
    pairs = []
    for g in range(256):
        core, z, yh, x, yl = coords(g)
        pairs.append((g, flat(core ^ dcore, z ^ dz, yh ^ dyh, x ^ dx, yl ^ dyl)))
    return pairs


def groups(key):
    found = {}
    for g in range(256):
        found.setdefault(key(*coords(g)), []).append(g)
    return [found[k] for k in sorted(found)]


CORE = swap(dcore=1)
Y_STEPS = ((1, 1), (1, 0), (0, 1))
GROUPS_Z = groups(lambda core, z, yh, x, yl: (core, yh, x, yl))
GROUPS_ZC = groups(lambda core, z, yh, x, yl: (yh, x, yl))
GROUPS_ZX = groups(lambda core, z, yh, x, yl: (core, yh, yl))


def exchange(value, group):
    return lax.all_to_all(value, BOTH, 0, 0, axis_index_groups=group, tiled=True)


VM = pl.BlockSpec(memory_space=pltpu.VMEM)
SM = pl.BlockSpec(memory_space=pltpu.SMEM)
HBM = pl.BlockSpec(memory_space=pltpu.HBM)


def call(body, out_shape, specs, name, scratch=(), limit=8):
    return pl.pallas_call(
        body,
        out_shape=out_shape,
        in_specs=specs,
        out_specs=jax.tree.map(lambda _: VM, out_shape),
        scratch_shapes=list(scratch),
        compiler_params=pltpu.CompilerParams(vmem_limit_bytes=limit * MIB),
        name=name,
    )


def shape(dims, dtype=F32):
    return jax.ShapeDtypeStruct(dims, dtype)


def down(row):
    return jnp.transpose(jnp.broadcast_to(row, (128, 128)))


def across(block):
    return jnp.sum(jnp.transpose(block), axis=0, keepdims=True)


def swapped(rows, step):
    return jnp.concatenate([rows[k ^ step : (k ^ step) + 1] for k in range(8)], axis=0)


def inv_norms(protos):
    wide = protos.astype(F32)
    return SLOPE * lax.rsqrt(jnp.sum(wide * wide, axis=0, keepdims=True) + 1e-06)


def unit(values):
    return (values * lax.rsqrt(jnp.sum(values * values, -1, keepdims=True) + 1e-06)).astype(BF16)


def units_body(feat_ref, mask_ref, unit_ref):
    for image in range(4):
        pick = lax.broadcasted_iota(jnp.int32, (256, 64), 0) == mask_ref[image : image + 1, :]
        chosen = lax.dot_general(
            pick.astype(BF16), feat_ref[image], (((0,), (0,)), ((), ())), preferred_element_type=F32
        )
        unit_ref[image * 64 : image * 64 + 64, :] = unit(chosen)


def send_body(where_ref, unit_ref, cls_ref, a_ref, b_ref, c_ref, send_ref):
    core, yh = where_ref[0], where_ref[2]
    half = unit_ref[pl.ds(pl.multiple_of(where_ref[4] * 128, 128), 128), :]
    cls = [unit(ref[...].astype(F32)).astype(F32) for ref in (cls_ref, a_ref, b_ref, c_ref)]
    near = [jnp.where(core == 0, cls[0], cls[1]), jnp.where(core == 0, cls[1], cls[0])]
    far = [jnp.where(core == 0, cls[2], cls[3]), jnp.where(core == 0, cls[3], cls[2])]
    first = [jnp.where(yh == 0, n, f) for n, f in zip(near, far)]
    second = [jnp.where(yh == 0, f, n) for n, f in zip(near, far)]
    tail = jnp.concatenate(first + second, axis=0).astype(BF16)
    for z in range(NZ):
        send_ref[z, :128, :] = half
        send_ref[z, 128:, :] = tail


def kernel_body(units_ref, *refs):
    pieces, (kern_ref, sums_ref) = refs[:8], refs[8:]
    for k in range(8):
        for half in range(2):
            lanes = slice(half * 256, half * 256 + 256)
            protos = pieces[k][:, lanes]
            scale = inv_norms(protos)
            total = jnp.zeros((8, 256), F32)
            for part in range(2):
                units = units_ref[part * 4 : part * 4 + 4, :128, :].reshape(512, 384)
                dots = jnp.dot(units, protos, preferred_element_type=F32)
                value = jnp.exp2(dots * scale - SLOPE)
                at = k * 512 + half * 256
                kern_ref[part * 512 : part * 512 + 512, at : at + 256] = value
                total = total + jnp.sum(value.reshape(64, 8, 256), axis=0)
            sums_ref[k : k + 1, lanes] = jnp.sum(total, axis=0, keepdims=True)


def cls_step(cls_kern, row_scale):
    wide = down(row_scale)
    cols = [
        1.0 / jnp.sum(cls_kern[:, q * 128 : q * 128 + 128] * wide, axis=0, keepdims=True)
        for q in range(4)
    ]
    total = cls_kern[:, :128] * cols[0]
    for q in range(1, 4):
        total = total + cls_kern[:, q * 128 : q * 128 + 128] * cols[q]
    return cols, across(total)


def cls_body(units_ref, protos_ref, sums_ref, kern_ref, message_ref):
    units = jnp.concatenate([units_ref[z, 128:, :] for z in range(NZ)], axis=0)
    protos = protos_ref[...]
    dots = jnp.dot(units, protos, preferred_element_type=F32)
    kern_ref[...] = jnp.exp2(dots * inv_norms(protos) - SLOPE)
    _, sums = cls_step(kern_ref[...], jnp.ones((1, 128), F32))
    message_ref[:, :512] = sums_ref[...]
    message_ref[:, 512:] = jnp.broadcast_to(sums, (8, 128))


def columns_body(last, got_ref, kern_ref, cls_kern_ref, message_ref, *more):
    total = got_ref[0]
    for k in range(1, 32):
        total = total + got_ref[k]
    row_scale = 1.0 / total[:9]
    cls_kern = cls_kern_ref[...]
    cols, sums = cls_step(cls_kern, row_scale[8:9])
    if last:
        for q in range(4):
            scaled = cls_kern[:, q * 128 : q * 128 + 128] * cols[q]
            for n in range(32):
                z, yh, core = n // 4, (n // 2) % 2, n % 2
                more[0][(yh * NZ + z) * 2 + core, :, q * 128 : q * 128 + 128] = scaled[n * 4 : n * 4 + 4]
    acc = more[-1]
    for z in range(NZ):
        wide = down(row_scale[z : z + 1]).reshape(16, 8, 128)
        for t in range(32):
            block = kern_ref[z * 128 : z * 128 + 128, t * 128 : t * 128 + 128]
            part = jnp.sum(block.reshape(16, 8, 128) * wide, axis=0)
            if z == 0:
                acc[:, t * 128 : t * 128 + 128] = part
            else:
                acc[:, t * 128 : t * 128 + 128] += part
    for k in range(8):
        message_ref[k : k + 1, :512] = jnp.sum(acc[:, k * 512 : k * 512 + 512], axis=0, keepdims=True)
    message_ref[:, 512:] = jnp.broadcast_to(sums, (8, 128))


def add_body(mine_ref, other_ref, out_ref):
    out_ref[...] = mine_ref[...] + swapped(other_ref[...], 4)


def rows_body(last, mine_ref, a_ref, b_ref, c_ref, kern_ref, send_ref, wide_ref):
    total = mine_ref[...]
    for ref, (dyh, dyl) in zip((a_ref, b_ref, c_ref), Y_STEPS):
        total = total + swapped(ref[...], dyh * 2 + dyl)
    cols = 1.0 / total[:, :512]
    cls = total[:1, 512:]
    for k in range(8):
        wide_ref[:, k * 512 : k * 512 + 512] = jnp.broadcast_to(cols[k : k + 1], (8, 512))
    sums = []
    for z in range(NZ):
        acc = jnp.zeros((16, 8, 128), F32)
        for t in range(32):
            block = kern_ref[z * 128 : z * 128 + 128, t * 128 : t * 128 + 128]
            acc = acc + block.reshape(16, 8, 128) * wide_ref[:, t * 128 : t * 128 + 128][None]
        sums.append(across(acc.reshape(128, 128)))
    if last:
        own = [cols[k : k + 1, q * 128 : q * 128 + 128] for k in (0, 2, 4, 6) for q in range(4)]
        own = jnp.concatenate(own, axis=0)
        rest = jnp.zeros((6, 128), F32)
        for z in range(NZ):
            block = jnp.concatenate([own, sums[z], cls, rest], axis=0)
            for x in range(NX):
                send_ref[z * NX + x] = block
    else:
        block = jnp.concatenate(sums + [cls, jnp.zeros((7, 128), F32)], axis=0)
        for k in range(32):
            send_ref[k] = block


def settle_body(where_ref, got_ref, cols_ref, sums_ref):
    core, yh, x = where_ref[0], where_ref[2], where_ref[3]
    total = got_ref[0, 16:24, :]
    for k in range(1, 32):
        total = total + got_ref[k, 16:24, :]
    sums_ref[...] = total
    for z in range(NZ):
        for cr in range(2):
            for yr in range(2):
                row = (jnp.bitwise_xor(yh, yr) * NZ + z) * 2 + jnp.bitwise_xor(core, cr)
                for q in range(4):
                    at = (cr * 2 + yr) * 4 + q
                    cols_ref[row, :, q * 128 : q * 128 + 128] = got_ref[z * NX + x, at : at + 1, :]


def cls_final_body(where_ref, scaled_ref, sums_ref, out_ref):
    base = ((where_ref[1] * 2 + where_ref[2]) * 2 + where_ref[0]) * 4
    scale = PROTOS / sums_ref[1:2, :]
    lane = lax.broadcasted_iota(jnp.int32, (1, 128), 1)
    rows = [jnp.sum(jnp.where(lane == base + v, scale, 0.0), axis=1, keepdims=True) for v in range(4)]
    scale = jnp.concatenate(rows, axis=0)
    for d in range(32):
        out_ref[:, d * 512 : d * 512 + 512] = (scaled_ref[d] * scale).astype(BF16)


PARTS = 8


def final_body(
    where_ref, near_ref, far_ref, units_ref, cols_ref, mine_ref, other_ref, out_ref, wide_ref, in_ref, stage_ref, in_sems, out_sems
):
    yh, yl = where_ref[2], where_ref[4]
    ins, outs, begins = [], [], []
    for n in range(PARTS):
        source = near_ref if n < PARTS // 2 else far_ref
        part = n % (PARTS // 2)
        begin = (yh if n < PARTS // 2 else 1 - yh) * 16 + part * 4
        lanes = pl.ds(pl.multiple_of(begin * 512, 2048), 2048)
        begins.append(begin)
        ins.append(pltpu.make_async_copy(source.at[pl.ds(part * 4, 4)], in_ref.at[n], in_sems.at[n]))
        outs.append(pltpu.make_async_copy(stage_ref.at[n], out_ref.at[:, lanes], out_sems.at[n]))
    for copy in ins:
        copy.start()
    mine, other = mine_ref[:1], other_ref[:1]
    wide_ref[:128] = PROTOS / down(jnp.where(yl == 0, mine, other))
    wide_ref[128:] = PROTOS / down(jnp.where(yl == 0, other, mine))
    for n in range(PARTS):
        ins[n].wait()
        for piece in range(4):
            for at in (0, 256):
                protos = in_ref[n, piece, :, at : at + 256]
                cols = cols_ref[begins[n] + piece][:, at : at + 256]
                dots = jnp.dot(units_ref[...], protos, preferred_element_type=F32)
                value = jnp.exp2(dots * inv_norms(protos) - SLOPE) * cols
                for q in (0, 128):
                    scaled = value[:, q : q + 128] * wide_ref[...]
                    to = piece * 512 + at + q
                    stage_ref[n, :, to : to + 128] = scaled.astype(BF16)
        outs[n].start()
    for copy in outs:
        copy.wait()


def final(where, near, far, units, cols, mine, other):
    return pl.pallas_call(
        final_body,
        out_shape=shape((256, 16384), BF16),
        in_specs=[SM, HBM, HBM, VM, VM, VM, VM],
        out_specs=pl.BlockSpec(memory_space=pl.ANY),
        scratch_shapes=[
            pltpu.VMEM((256, 128), F32),
            pltpu.VMEM((PARTS, 4, 384, 512), BF16),
            pltpu.VMEM((PARTS, 256, 2048), BF16),
            pltpu.SemaphoreType.DMA((PARTS,)),
            pltpu.SemaphoreType.DMA((PARTS,)),
        ],
        compiler_params=pltpu.CompilerParams(vmem_limit_bytes=56 * MIB),
        name="final_scale",
    )(where, near, far, units, cols, mine, other)


def per_device(cls_features, patch_features, mask_index, cls_protos, patch_protos):
    dp, proto = lax.axis_index("dp"), lax.axis_index("proto")
    core, z, yh = dp % 2, (dp // 2) % NZ, dp // (2 * NZ)
    x, yl = proto % NX, proto // NX
    where = jnp.stack([core, z, yh, x, yl]).astype(jnp.int32)

    cls_near = [lax.ppermute(cls_features, BOTH, swap(dcore=c, dyh=h)) for c, h in ((1, 0), (0, 1), (1, 1))]

    near = {(0, 0): patch_protos}
    for dyh, dyl in Y_STEPS:
        near[dyh, dyl] = lax.ppermute(patch_protos, BOTH, swap(dyh=dyh, dyl=dyl))
    pieces = [near[k // 2, k % 2] for k in range(4)]
    pieces += [lax.ppermute(piece, BOTH, CORE) for piece in pieces]

    units = call(units_body, shape((256, 384), BF16), [VM] * 2, "units")(patch_features, mask_index)
    send = call(send_body, shape((NZ, 144, 384), BF16), [SM] + [VM] * 5, "send")(where, units, cls_features, *cls_near)
    rows = exchange(send, GROUPS_Z)

    held = lax.optimization_barrier((patch_protos, near[1, 0], rows, near[0, 1], near[1, 1]))[:2]
    gathered = [lax.all_gather(piece, BOTH, axis_index_groups=GROUPS_ZC) for piece in held]

    kern, col_sums = call(
        kernel_body, (pltpu.VMEM((1024, 4096), F32), shape((8, 512))), [VM] * 9, "patch_kernel"
    )(rows, *pieces)
    cls_kern, message = call(cls_body, (shape((128, 512)), shape((8, 640))), [VM] * 3, "cls_kernel")(
        rows, cls_protos, col_sums
    )

    for step in range(ITERS):
        last = step == ITERS - 1
        if step:
            outs = [shape((8, 640))]
            if last:
                outs.append(shape((32, 4, 512)))
            done = call(
                functools.partial(columns_body, last),
                tuple(outs),
                [VM] * 3,
                "column_sums",
                [pltpu.VMEM((8, 4096), F32)],
            )(got, kern, cls_kern)
            message = done[0]
        message = call(add_body, shape((8, 640)), [VM] * 2, "add_core")(message, lax.ppermute(message, BOTH, CORE))
        parts = [lax.ppermute(message, BOTH, swap(dyh=dyh, dyl=dyl)) for dyh, dyl in Y_STEPS]
        send = call(
            functools.partial(rows_body, last),
            shape((32, 24 if last else 16, 128)),
            [VM] * 5,
            "row_sums",
            [pltpu.VMEM((8, 4096), F32)],
        )(message, *parts, kern)
        got = exchange(send, GROUPS_ZX)

    cols, sums = call(settle_body, (shape((32, 1, 512)), shape((8, 128))), [SM, VM], "settle")(where, got)
    cls_scaled = lax.optimization_barrier((done[1], sums))[0]
    cls_scaled = lax.all_to_all(cls_scaled, "dp", 0, 0, tiled=True)
    other = lax.ppermute(sums, BOTH, swap(dyl=1))
    patch_targets = final(where, *gathered, units, cols, sums, other)
    cls_scaled, patch_targets = lax.optimization_barrier((cls_scaled, patch_targets))
    cls_targets = call(cls_final_body, shape((4, 16384), BF16), [SM, VM, VM], "cls_final")(where, cls_scaled, sums)
    return (cls_targets, patch_targets)


def solution(mesh):
    return jax.shard_map(
        per_device,
        mesh=mesh,
        in_specs=(
            P("dp", None),
            P("dp", None, None),
            P("dp", None),
            P(None, ("proto", "dp")),
            P(None, ("proto", "dp")),
        ),
        out_specs=(P("dp", "proto"), P("dp", "proto")),
        check_vma=False,
    )
```

```python
import functools

import jax
import jax.numpy as jnp
import numpy as np
from jax import lax
from jax.experimental import pallas as pl
from jax.experimental.pallas import tpu as pltpu
from jax.sharding import PartitionSpec as P

PROTOS = 131072
ITERS = 3
TEMP = 0.07
SLOPE = float(1.0 / (TEMP * np.log(2.0)))
F32 = jnp.float32
BF16 = jnp.bfloat16
BOTH = ("dp", "proto")
MIB = 1 << 20

NZ, NX = 8, 4


def coords(g):
    d, p = g // 8, g % 8
    return d % 2, (d // 2) % NZ, d // (2 * NZ), p % NX, p // NX


def flat(core, z, yh, x, yl):
    return ((yh * NZ + z) * 2 + core) * 8 + yl * NX + x


def swap(dcore=0, dz=0, dyh=0, dx=0, dyl=0):
    pairs = []
    for g in range(256):
        core, z, yh, x, yl = coords(g)
        pairs.append((g, flat(core ^ dcore, z ^ dz, yh ^ dyh, x ^ dx, yl ^ dyl)))
    return pairs


def groups(key):
    found = {}
    for g in range(256):
        found.setdefault(key(*coords(g)), []).append(g)
    return [found[k] for k in sorted(found)]


CORE = swap(dcore=1)
Y_STEPS = ((1, 1), (1, 0), (0, 1))
GROUPS_Z = groups(lambda core, z, yh, x, yl: (core, yh, x, yl))
GROUPS_ZC = groups(lambda core, z, yh, x, yl: (yh, x, yl))
GROUPS_ZX = groups(lambda core, z, yh, x, yl: (core, yh, yl))


def exchange(value, group):
    return lax.all_to_all(value, BOTH, 0, 0, axis_index_groups=group, tiled=True)


VM = pl.BlockSpec(memory_space=pltpu.VMEM)
SM = pl.BlockSpec(memory_space=pltpu.SMEM)
HBM = pl.BlockSpec(memory_space=pltpu.HBM)


def call(body, out_shape, specs, name, scratch=(), limit=8):
    return pl.pallas_call(
        body,
        out_shape=out_shape,
        in_specs=specs,
        out_specs=jax.tree.map(lambda _: VM, out_shape),
        scratch_shapes=list(scratch),
        compiler_params=pltpu.CompilerParams(vmem_limit_bytes=limit * MIB),
        name=name,
    )


def shape(dims, dtype=F32):
    return jax.ShapeDtypeStruct(dims, dtype)


def down(row):
    return jnp.transpose(jnp.broadcast_to(row, (128, 128)))


def across(block):
    return jnp.sum(jnp.transpose(block), axis=0, keepdims=True)


def swapped(rows, step):
    return jnp.concatenate([rows[k ^ step : (k ^ step) + 1] for k in range(8)], axis=0)


def inv_norms(protos):
    wide = protos.astype(F32)
    return SLOPE * lax.rsqrt(jnp.sum(wide * wide, axis=0, keepdims=True) + 1e-06)


def unit(values):
    return (values * lax.rsqrt(jnp.sum(values * values, -1, keepdims=True) + 1e-06)).astype(BF16)


def units_body(feat_ref, mask_ref, unit_ref):
    for image in range(4):
        pick = lax.broadcasted_iota(jnp.int32, (256, 64), 0) == mask_ref[image : image + 1, :]
        chosen = lax.dot_general(
            pick.astype(BF16), feat_ref[image], (((0,), (0,)), ((), ())), preferred_element_type=F32
        )
        unit_ref[image * 64 : image * 64 + 64, :] = unit(chosen)


def send_body(where_ref, unit_ref, cls_ref, a_ref, b_ref, c_ref, send_ref):
    core, yh = where_ref[0], where_ref[2]
    half = unit_ref[pl.ds(pl.multiple_of(where_ref[4] * 128, 128), 128), :]
    cls = [unit(ref[...].astype(F32)).astype(F32) for ref in (cls_ref, a_ref, b_ref, c_ref)]
    near = [jnp.where(core == 0, cls[0], cls[1]), jnp.where(core == 0, cls[1], cls[0])]
    far = [jnp.where(core == 0, cls[2], cls[3]), jnp.where(core == 0, cls[3], cls[2])]
    first = [jnp.where(yh == 0, n, f) for n, f in zip(near, far)]
    second = [jnp.where(yh == 0, f, n) for n, f in zip(near, far)]
    tail = jnp.concatenate(first + second, axis=0).astype(BF16)
    for z in range(NZ):
        send_ref[z, :128, :] = half
        send_ref[z, 128:, :] = tail


def cls_step(cls_kern, row_scale):
    wide = down(row_scale)
    cols = [
        1.0 / jnp.sum(cls_kern[:, q * 128 : q * 128 + 128] * wide, axis=0, keepdims=True)
        for q in range(4)
    ]
    total = cls_kern[:, :128] * cols[0]
    for q in range(1, 4):
        total = total + cls_kern[:, q * 128 : q * 128 + 128] * cols[q]
    return cols, across(total)


def kernel_body(rows_ref, cls_ref, *refs):
    pieces, (kern_ref, cls_kern_ref, message_ref, units_ref, held_ref, sems) = refs[:8], refs[8:]
    copies = [pltpu.make_async_copy(rows_ref, units_ref, sems.at[9])]
    copies += [pltpu.make_async_copy(ref, held_ref.at[k], sems.at[k]) for k, ref in enumerate((*pieces, cls_ref))]
    for copy in copies:
        copy.start()
    copies[0].wait()
    for k in range(8):
        copies[k + 1].wait()
        for half in range(2):
            lanes = slice(half * 256, half * 256 + 256)
            protos = held_ref[k, :, lanes]
            scale = inv_norms(protos)
            total = jnp.zeros((8, 256), F32)
            for part in range(2):
                units = units_ref[part * 4 : part * 4 + 4, :128, :].reshape(512, 384)
                dots = jnp.dot(units, protos, preferred_element_type=F32)
                value = jnp.exp2(dots * scale - SLOPE)
                at = k * 512 + half * 256
                kern_ref[part * 512 : part * 512 + 512, at : at + 256] = value
                total = total + jnp.sum(value.reshape(64, 8, 256), axis=0)
            message_ref[k : k + 1, lanes] = jnp.sum(total, axis=0, keepdims=True)
    copies[9].wait()
    units = jnp.concatenate([units_ref[z, 128:, :] for z in range(NZ)], axis=0)
    protos = held_ref[8]
    dots = jnp.dot(units, protos, preferred_element_type=F32)
    cls_kern_ref[...] = jnp.exp2(dots * inv_norms(protos) - SLOPE)
    _, sums = cls_step(cls_kern_ref[...], jnp.ones((1, 128), F32))
    message_ref[:, 512:] = jnp.broadcast_to(sums, (8, 128))


def columns_body(last, got_ref, kern_ref, cls_kern_ref, message_ref, *more):
    total = got_ref[0]
    for k in range(1, 32):
        total = total + got_ref[k]
    row_scale = 1.0 / total[:9]
    cls_kern = cls_kern_ref[...]
    cols, sums = cls_step(cls_kern, row_scale[8:9])
    if last:
        for q in range(4):
            scaled = cls_kern[:, q * 128 : q * 128 + 128] * cols[q]
            for n in range(32):
                z, yh, core = n // 4, (n // 2) % 2, n % 2
                more[0][(yh * NZ + z) * 2 + core, :, q * 128 : q * 128 + 128] = scaled[n * 4 : n * 4 + 4]
    acc = more[-1]
    for z in range(NZ):
        wide = down(row_scale[z : z + 1]).reshape(16, 8, 128)
        for t in range(32):
            block = kern_ref[z * 128 : z * 128 + 128, t * 128 : t * 128 + 128]
            part = jnp.sum(block.reshape(16, 8, 128) * wide, axis=0)
            if z == 0:
                acc[:, t * 128 : t * 128 + 128] = part
            else:
                acc[:, t * 128 : t * 128 + 128] += part
    for k in range(8):
        message_ref[k : k + 1, :512] = jnp.sum(acc[:, k * 512 : k * 512 + 512], axis=0, keepdims=True)
    message_ref[:, 512:] = jnp.broadcast_to(sums, (8, 128))


def add_body(mine_ref, other_ref, out_ref):
    out_ref[...] = mine_ref[...] + swapped(other_ref[...], 4)


def rows_body(last, mine_ref, a_ref, b_ref, c_ref, kern_ref, send_ref, wide_ref):
    total = mine_ref[...]
    for ref, (dyh, dyl) in zip((a_ref, b_ref, c_ref), Y_STEPS):
        total = total + swapped(ref[...], dyh * 2 + dyl)
    cols = 1.0 / total[:, :512]
    cls = total[:1, 512:]
    for k in range(8):
        wide_ref[:, k * 512 : k * 512 + 512] = jnp.broadcast_to(cols[k : k + 1], (8, 512))
    sums = []
    for z in range(NZ):
        acc = jnp.zeros((16, 8, 128), F32)
        for t in range(32):
            block = kern_ref[z * 128 : z * 128 + 128, t * 128 : t * 128 + 128]
            acc = acc + block.reshape(16, 8, 128) * wide_ref[:, t * 128 : t * 128 + 128][None]
        sums.append(across(acc.reshape(128, 128)))
    if last:
        own = [cols[k : k + 1, q * 128 : q * 128 + 128] for k in (0, 2, 4, 6) for q in range(4)]
        own = jnp.concatenate(own, axis=0)
        rest = jnp.zeros((6, 128), F32)
        for z in range(NZ):
            block = jnp.concatenate([own, sums[z], cls, rest], axis=0)
            for x in range(NX):
                send_ref[z * NX + x] = block
    else:
        block = jnp.concatenate(sums + [cls, jnp.zeros((7, 128), F32)], axis=0)
        for k in range(32):
            send_ref[k] = block


def settle_body(where_ref, got_ref, cols_ref, sums_ref):
    core, yh, x = where_ref[0], where_ref[2], where_ref[3]
    total = got_ref[0, 16:24, :]
    for k in range(1, 32):
        total = total + got_ref[k, 16:24, :]
    sums_ref[...] = total
    for z in range(NZ):
        for cr in range(2):
            for yr in range(2):
                row = (jnp.bitwise_xor(yh, yr) * NZ + z) * 2 + jnp.bitwise_xor(core, cr)
                for q in range(4):
                    at = (cr * 2 + yr) * 4 + q
                    cols_ref[row, :, q * 128 : q * 128 + 128] = got_ref[z * NX + x, at : at + 1, :]


def cls_final_body(where_ref, scaled_ref, sums_ref, out_ref):
    base = ((where_ref[1] * 2 + where_ref[2]) * 2 + where_ref[0]) * 4
    scale = PROTOS / sums_ref[1:2, :]
    lane = lax.broadcasted_iota(jnp.int32, (1, 128), 1)
    rows = [jnp.sum(jnp.where(lane == base + v, scale, 0.0), axis=1, keepdims=True) for v in range(4)]
    scale = jnp.concatenate(rows, axis=0)
    for d in range(32):
        out_ref[:, d * 512 : d * 512 + 512] = (scaled_ref[d] * scale).astype(BF16)


PARTS = 8


def final_body(
    where_ref, near_ref, far_ref, units_ref, cols_ref, mine_ref, other_ref, out_ref, wide_ref, in_ref, stage_ref, in_sems, out_sems
):
    yh, yl = where_ref[2], where_ref[4]
    ins, outs, begins = [], [], []
    for n in range(PARTS):
        source = near_ref if n < PARTS // 2 else far_ref
        part = n % (PARTS // 2)
        begin = (yh if n < PARTS // 2 else 1 - yh) * 16 + part * 4
        lanes = pl.ds(pl.multiple_of(begin * 512, 2048), 2048)
        begins.append(begin)
        ins.append(pltpu.make_async_copy(source.at[pl.ds(part * 4, 4)], in_ref.at[n], in_sems.at[n]))
        outs.append(pltpu.make_async_copy(stage_ref.at[n], out_ref.at[:, lanes], out_sems.at[n]))
    for copy in ins:
        copy.start()
    mine, other = mine_ref[:1], other_ref[:1]
    wide_ref[:128] = PROTOS / down(jnp.where(yl == 0, mine, other))
    wide_ref[128:] = PROTOS / down(jnp.where(yl == 0, other, mine))
    for n in range(PARTS):
        ins[n].wait()
        for piece in range(4):
            for at in (0, 256):
                protos = in_ref[n, piece, :, at : at + 256]
                cols = cols_ref[begins[n] + piece][:, at : at + 256]
                dots = jnp.dot(units_ref[...], protos, preferred_element_type=F32)
                value = jnp.exp2(dots * inv_norms(protos) - SLOPE) * cols
                for q in (0, 128):
                    scaled = value[:, q : q + 128] * wide_ref[...]
                    to = piece * 512 + at + q
                    stage_ref[n, :, to : to + 128] = scaled.astype(BF16)
        outs[n].start()
    for copy in outs:
        copy.wait()


def final(where, near, far, units, cols, mine, other):
    return pl.pallas_call(
        final_body,
        out_shape=shape((256, 16384), BF16),
        in_specs=[SM, HBM, HBM, VM, VM, VM, VM],
        out_specs=pl.BlockSpec(memory_space=pl.ANY),
        scratch_shapes=[
            pltpu.VMEM((256, 128), F32),
            pltpu.VMEM((PARTS, 4, 384, 512), BF16),
            pltpu.VMEM((PARTS, 256, 2048), BF16),
            pltpu.SemaphoreType.DMA((PARTS,)),
            pltpu.SemaphoreType.DMA((PARTS,)),
        ],
        compiler_params=pltpu.CompilerParams(vmem_limit_bytes=50 * MIB),
        name="final_scale",
    )(where, near, far, units, cols, mine, other)


def per_device(cls_features, patch_features, mask_index, cls_protos, patch_protos):
    dp, proto = lax.axis_index("dp"), lax.axis_index("proto")
    core, z, yh = dp % 2, (dp // 2) % NZ, dp // (2 * NZ)
    x, yl = proto % NX, proto // NX
    where = jnp.stack([core, z, yh, x, yl]).astype(jnp.int32)

    cls_near = [lax.ppermute(cls_features, BOTH, swap(dcore=c, dyh=h)) for c, h in ((1, 0), (0, 1), (1, 1))]

    near = {(0, 0): patch_protos}
    for dyh, dyl in Y_STEPS:
        near[dyh, dyl] = lax.ppermute(patch_protos, BOTH, swap(dyh=dyh, dyl=dyl))
    pieces = [near[k // 2, k % 2] for k in range(4)]
    pieces += [lax.ppermute(piece, BOTH, CORE) for piece in pieces]

    units = call(units_body, shape((256, 384), BF16), [VM] * 2, "units")(patch_features, mask_index)
    send = call(send_body, shape((NZ, 144, 384), BF16), [SM] + [VM] * 5, "send")(where, units, cls_features, *cls_near)
    rows = exchange(send, GROUPS_Z)

    held = lax.optimization_barrier((patch_protos, near[1, 0], rows, *pieces[1:2], *pieces[3:]))[:2]
    gathered = [lax.all_gather(piece, BOTH, axis_index_groups=GROUPS_ZC) for piece in held]

    kern, cls_kern, message = call(
        kernel_body,
        (pltpu.VMEM((1024, 4096), F32), shape((128, 512)), shape((8, 640))),
        [HBM] * 10,
        "patch_kernel",
        [
            pltpu.VMEM((NZ, 144, 384), BF16),
            pltpu.VMEM((9, 384, 512), BF16),
            pltpu.SemaphoreType.DMA((10,)),
        ],
        limit=43,
    )(rows, cls_protos, *pieces)

    for step in range(ITERS):
        last = step == ITERS - 1
        if step:
            outs = [shape((8, 640))]
            if last:
                outs.append(shape((32, 4, 512)))
            done = call(
                functools.partial(columns_body, last),
                tuple(outs),
                [VM] * 3,
                "column_sums",
                [pltpu.VMEM((8, 4096), F32)],
            )(got, kern, cls_kern)
            message = done[0]
        message = call(add_body, shape((8, 640)), [VM] * 2, "add_core")(message, lax.ppermute(message, BOTH, CORE))
        parts = [lax.ppermute(message, BOTH, swap(dyh=dyh, dyl=dyl)) for dyh, dyl in Y_STEPS]
        send = call(
            functools.partial(rows_body, last),
            shape((32, 24 if last else 16, 128)),
            [VM] * 5,
            "row_sums",
            [pltpu.VMEM((8, 4096), F32)],
        )(message, *parts, kern)
        got = exchange(send, GROUPS_ZX)

    cols, sums = call(settle_body, (shape((32, 1, 512)), shape((8, 128))), [SM, VM], "settle")(where, got)
    cls_scaled = lax.optimization_barrier((done[1], sums))[0]
    cls_scaled = lax.all_to_all(cls_scaled, "dp", 0, 0, tiled=True)
    other = lax.ppermute(sums, BOTH, swap(dyl=1))
    patch_targets = final(where, *gathered, units, cols, sums, other)
    cls_scaled, patch_targets = lax.optimization_barrier((cls_scaled, patch_targets))
    cls_targets = call(cls_final_body, shape((4, 16384), BF16), [SM, VM, VM], "cls_final")(where, cls_scaled, sums)
    return (cls_targets, patch_targets)


def solution(mesh):
    return jax.shard_map(
        per_device,
        mesh=mesh,
        in_specs=(
            P("dp", None),
            P("dp", None, None),
            P("dp", None),
            P(None, ("proto", "dp")),
            P(None, ("proto", "dp")),
        ),
        out_specs=(P("dp", "proto"), P("dp", "proto")),
        check_vma=False,
    )
```

```python
import functools

import jax
import jax.numpy as jnp
import numpy as np
from jax import lax
from jax.experimental import pallas as pl
from jax.experimental.pallas import tpu as pltpu
from jax.sharding import PartitionSpec as P

PROTOS = 131072
ITERS = 3
TEMP = 0.07
SLOPE = float(1.0 / (TEMP * np.log(2.0)))
F32 = jnp.float32
BF16 = jnp.bfloat16
BOTH = ("dp", "proto")
MIB = 1 << 20

NZ, NX = 8, 4


def coords(g):
    d, p = g // 8, g % 8
    return d % 2, (d // 2) % NZ, d // (2 * NZ), p % NX, p // NX


def flat(core, z, yh, x, yl):
    return ((yh * NZ + z) * 2 + core) * 8 + yl * NX + x


def swap(dcore=0, dz=0, dyh=0, dx=0, dyl=0):
    pairs = []
    for g in range(256):
        core, z, yh, x, yl = coords(g)
        pairs.append((g, flat(core ^ dcore, z ^ dz, yh ^ dyh, x ^ dx, yl ^ dyl)))
    return pairs


def groups(key):
    found = {}
    for g in range(256):
        found.setdefault(key(*coords(g)), []).append(g)
    return [found[k] for k in sorted(found)]


CORE = swap(dcore=1)
Y_STEPS = ((1, 1), (1, 0), (0, 1))
GROUPS_Z = groups(lambda core, z, yh, x, yl: (core, yh, x, yl))
GROUPS_ZC = groups(lambda core, z, yh, x, yl: (yh, x, yl))
GROUPS_ZX = groups(lambda core, z, yh, x, yl: (core, yh, yl))


def exchange(value, group):
    return lax.all_to_all(value, BOTH, 0, 0, axis_index_groups=group, tiled=True)


VM = pl.BlockSpec(memory_space=pltpu.VMEM)
SM = pl.BlockSpec(memory_space=pltpu.SMEM)
HBM = pl.BlockSpec(memory_space=pltpu.HBM)


def call(body, out_shape, specs, name, scratch=(), limit=8):
    return pl.pallas_call(
        body,
        out_shape=out_shape,
        in_specs=specs,
        out_specs=jax.tree.map(lambda _: VM, out_shape),
        scratch_shapes=list(scratch),
        compiler_params=pltpu.CompilerParams(vmem_limit_bytes=limit * MIB),
        name=name,
    )


def shape(dims, dtype=F32):
    return jax.ShapeDtypeStruct(dims, dtype)


def down(row):
    return jnp.transpose(jnp.broadcast_to(row, (128, 128)))


def across(block):
    return jnp.sum(jnp.transpose(block), axis=0, keepdims=True)


def swapped(rows, step):
    return jnp.concatenate([rows[k ^ step : (k ^ step) + 1] for k in range(8)], axis=0)


def inv_norms(protos):
    wide = protos.astype(F32)
    return SLOPE * lax.rsqrt(jnp.sum(wide * wide, axis=0, keepdims=True) + 1e-06)


def unit(values):
    return (values * lax.rsqrt(jnp.sum(values * values, -1, keepdims=True) + 1e-06)).astype(BF16)


def units_body(feat_ref, mask_ref, unit_ref):
    for image in range(4):
        pick = lax.broadcasted_iota(jnp.int32, (256, 64), 0) == mask_ref[image : image + 1, :]
        chosen = lax.dot_general(
            pick.astype(BF16), feat_ref[image], (((0,), (0,)), ((), ())), preferred_element_type=F32
        )
        unit_ref[image * 64 : image * 64 + 64, :] = unit(chosen)


def send_body(where_ref, unit_ref, cls_ref, a_ref, b_ref, c_ref, send_ref):
    core, yh = where_ref[0], where_ref[2]
    half = unit_ref[pl.ds(pl.multiple_of(where_ref[4] * 128, 128), 128), :]
    cls = [unit(ref[...].astype(F32)).astype(F32) for ref in (cls_ref, a_ref, b_ref, c_ref)]
    near = [jnp.where(core == 0, cls[0], cls[1]), jnp.where(core == 0, cls[1], cls[0])]
    far = [jnp.where(core == 0, cls[2], cls[3]), jnp.where(core == 0, cls[3], cls[2])]
    first = [jnp.where(yh == 0, n, f) for n, f in zip(near, far)]
    second = [jnp.where(yh == 0, f, n) for n, f in zip(near, far)]
    tail = jnp.concatenate(first + second, axis=0).astype(BF16)
    send_ref[:128, :] = half
    send_ref[128:, :] = tail


def cls_step(cls_kern, row_scale):
    wide = down(row_scale)
    cols = [
        1.0 / jnp.sum(cls_kern[:, q * 128 : q * 128 + 128] * wide, axis=0, keepdims=True)
        for q in range(4)
    ]
    total = cls_kern[:, :128] * cols[0]
    for q in range(1, 4):
        total = total + cls_kern[:, q * 128 : q * 128 + 128] * cols[q]
    return cols, across(total)


def kernel_body(units_ref, cls_ref, *refs):
    pieces, (kern_ref, cls_kern_ref, message_ref) = refs[:8], refs[8:]
    for k in range(8):
        for half in range(2):
            lanes = slice(half * 256, half * 256 + 256)
            protos = pieces[k][:, lanes]
            scale = inv_norms(protos)
            total = jnp.zeros((8, 256), F32)
            for part in range(2):
                units = units_ref[part * 4 : part * 4 + 4, :128, :].reshape(512, 384)
                dots = jnp.dot(units, protos, preferred_element_type=F32)
                value = jnp.exp2(dots * scale - SLOPE)
                at = k * 512 + half * 256
                kern_ref[part * 512 : part * 512 + 512, at : at + 256] = value
                total = total + jnp.sum(value.reshape(64, 8, 256), axis=0)
            message_ref[k : k + 1, lanes] = jnp.sum(total, axis=0, keepdims=True)
    units = jnp.concatenate([units_ref[z, 128:, :] for z in range(NZ)], axis=0)
    protos = cls_ref[...]
    dots = jnp.dot(units, protos, preferred_element_type=F32)
    cls_kern_ref[...] = jnp.exp2(dots * inv_norms(protos) - SLOPE)
    _, sums = cls_step(cls_kern_ref[...], jnp.ones((1, 128), F32))
    message_ref[:, 512:] = jnp.broadcast_to(sums, (8, 128))


def columns_body(last, got_ref, kern_ref, cls_kern_ref, message_ref, *more):
    total = got_ref[0]
    for k in range(1, 32):
        total = total + got_ref[k]
    row_scale = 1.0 / total[:9]
    cls_kern = cls_kern_ref[...]
    cols, sums = cls_step(cls_kern, row_scale[8:9])
    if last:
        for q in range(4):
            scaled = cls_kern[:, q * 128 : q * 128 + 128] * cols[q]
            for n in range(32):
                z, yh, core = n // 4, (n // 2) % 2, n % 2
                more[0][(yh * NZ + z) * 2 + core, :, q * 128 : q * 128 + 128] = scaled[n * 4 : n * 4 + 4]
    acc = more[-1]
    for z in range(NZ):
        wide = down(row_scale[z : z + 1]).reshape(16, 8, 128)
        for t in range(32):
            block = kern_ref[z * 128 : z * 128 + 128, t * 128 : t * 128 + 128]
            part = jnp.sum(block.reshape(16, 8, 128) * wide, axis=0)
            if z == 0:
                acc[:, t * 128 : t * 128 + 128] = part
            else:
                acc[:, t * 128 : t * 128 + 128] += part
    for k in range(8):
        message_ref[k : k + 1, :512] = jnp.sum(acc[:, k * 512 : k * 512 + 512], axis=0, keepdims=True)
    message_ref[:, 512:] = jnp.broadcast_to(sums, (8, 128))


def add_body(mine_ref, other_ref, out_ref):
    out_ref[...] = mine_ref[...] + swapped(other_ref[...], 4)


def rows_body(last, mine_ref, a_ref, b_ref, c_ref, kern_ref, send_ref, wide_ref):
    total = mine_ref[...]
    for ref, (dyh, dyl) in zip((a_ref, b_ref, c_ref), Y_STEPS):
        total = total + swapped(ref[...], dyh * 2 + dyl)
    cols = 1.0 / total[:, :512]
    cls = total[:1, 512:]
    for k in range(8):
        wide_ref[:, k * 512 : k * 512 + 512] = jnp.broadcast_to(cols[k : k + 1], (8, 512))
    sums = []
    for z in range(NZ):
        acc = jnp.zeros((16, 8, 128), F32)
        for t in range(32):
            block = kern_ref[z * 128 : z * 128 + 128, t * 128 : t * 128 + 128]
            acc = acc + block.reshape(16, 8, 128) * wide_ref[:, t * 128 : t * 128 + 128][None]
        sums.append(across(acc.reshape(128, 128)))
    if last:
        own = [cols[k : k + 1, q * 128 : q * 128 + 128] for k in (0, 2, 4, 6) for q in range(4)]
        own = jnp.concatenate(own, axis=0)
        rest = jnp.zeros((6, 128), F32)
        for z in range(NZ):
            block = jnp.concatenate([own, sums[z], cls, rest], axis=0)
            for x in range(NX):
                send_ref[z * NX + x] = block
    else:
        block = jnp.concatenate(sums + [cls, jnp.zeros((7, 128), F32)], axis=0)
        for k in range(32):
            send_ref[k] = block


def settle_body(where_ref, got_ref, cols_ref, sums_ref):
    core, yh, x = where_ref[0], where_ref[2], where_ref[3]
    total = got_ref[0, 16:24, :]
    for k in range(1, 32):
        total = total + got_ref[k, 16:24, :]
    sums_ref[...] = total
    for z in range(NZ):
        for cr in range(2):
            for yr in range(2):
                row = (jnp.bitwise_xor(yh, yr) * NZ + z) * 2 + jnp.bitwise_xor(core, cr)
                for q in range(4):
                    at = (cr * 2 + yr) * 4 + q
                    cols_ref[row, :, q * 128 : q * 128 + 128] = got_ref[z * NX + x, at : at + 1, :]


def cls_final_body(where_ref, scaled_ref, sums_ref, out_ref):
    base = ((where_ref[1] * 2 + where_ref[2]) * 2 + where_ref[0]) * 4
    scale = PROTOS / sums_ref[1:2, :]
    lane = lax.broadcasted_iota(jnp.int32, (1, 128), 1)
    rows = [jnp.sum(jnp.where(lane == base + v, scale, 0.0), axis=1, keepdims=True) for v in range(4)]
    scale = jnp.concatenate(rows, axis=0)
    for d in range(32):
        out_ref[:, d * 512 : d * 512 + 512] = (scaled_ref[d] * scale).astype(BF16)


PARTS = 8


def final_body(
    where_ref, near_ref, far_ref, units_ref, cols_ref, mine_ref, other_ref, out_ref, wide_ref, in_ref, stage_ref, in_sems, out_sems
):
    yh, yl = where_ref[2], where_ref[4]
    ins, outs, begins = [], [], []
    for n in range(PARTS):
        source = near_ref if n < PARTS // 2 else far_ref
        part = n % (PARTS // 2)
        begin = (yh if n < PARTS // 2 else 1 - yh) * 16 + part * 4
        lanes = pl.ds(pl.multiple_of(begin * 512, 2048), 2048)
        begins.append(begin)
        ins.append(pltpu.make_async_copy(source.at[pl.ds(part * 4, 4)], in_ref.at[n], in_sems.at[n]))
        outs.append(pltpu.make_async_copy(stage_ref.at[n], out_ref.at[:, lanes], out_sems.at[n]))
    for copy in ins:
        copy.start()
    mine, other = mine_ref[:1], other_ref[:1]
    wide_ref[:128] = PROTOS / down(jnp.where(yl == 0, mine, other))
    wide_ref[128:] = PROTOS / down(jnp.where(yl == 0, other, mine))
    for n in range(PARTS):
        ins[n].wait()
        for piece in range(4):
            for at in (0, 256):
                protos = in_ref[n, piece, :, at : at + 256]
                cols = cols_ref[begins[n] + piece][:, at : at + 256]
                dots = jnp.dot(units_ref[...], protos, preferred_element_type=F32)
                value = jnp.exp2(dots * inv_norms(protos) - SLOPE) * cols
                for q in (0, 128):
                    scaled = value[:, q : q + 128] * wide_ref[...]
                    to = piece * 512 + at + q
                    stage_ref[n, :, to : to + 128] = scaled.astype(BF16)
        outs[n].start()
    for copy in outs:
        copy.wait()


def final(where, near, far, units, cols, mine, other):
    return pl.pallas_call(
        final_body,
        out_shape=shape((256, 16384), BF16),
        in_specs=[SM, HBM, HBM, VM, VM, VM, VM],
        out_specs=pl.BlockSpec(memory_space=pl.ANY),
        scratch_shapes=[
            pltpu.VMEM((256, 128), F32),
            pltpu.VMEM((PARTS, 4, 384, 512), BF16),
            pltpu.VMEM((PARTS, 256, 2048), BF16),
            pltpu.SemaphoreType.DMA((PARTS,)),
            pltpu.SemaphoreType.DMA((PARTS,)),
        ],
        compiler_params=pltpu.CompilerParams(vmem_limit_bytes=50 * MIB),
        name="final_scale",
    )(where, near, far, units, cols, mine, other)


def per_device(cls_features, patch_features, mask_index, cls_protos, patch_protos):
    dp, proto = lax.axis_index("dp"), lax.axis_index("proto")
    core, z, yh = dp % 2, (dp // 2) % NZ, dp // (2 * NZ)
    x, yl = proto % NX, proto // NX
    where = jnp.stack([core, z, yh, x, yl]).astype(jnp.int32)

    cls_near = [lax.ppermute(cls_features, BOTH, swap(dcore=c, dyh=h)) for c, h in ((1, 0), (0, 1), (1, 1))]

    near = {(0, 0): patch_protos}
    for dyh, dyl in Y_STEPS:
        near[dyh, dyl] = lax.ppermute(patch_protos, BOTH, swap(dyh=dyh, dyl=dyl))

    units = call(units_body, shape((256, 384), BF16), [VM] * 2, "units")(patch_features, mask_index)
    send = call(send_body, shape((144, 384), BF16), [SM] + [VM] * 5, "send")(where, units, cls_features, *cls_near)
    rows = lax.all_gather(send, BOTH, axis_index_groups=GROUPS_Z)

    pieces = [near[k // 2, k % 2] for k in range(4)]
    pieces[1:] = lax.optimization_barrier((*pieces[1:], rows))[:3]
    pieces += [lax.ppermute(piece, BOTH, CORE) for piece in pieces]

    held = lax.optimization_barrier((patch_protos, pieces[2], rows, *pieces[1:2], *pieces[3:]))[:2]
    gathered = [lax.all_gather(piece, BOTH, axis_index_groups=GROUPS_ZC) for piece in held]

    kern, cls_kern, message = call(
        kernel_body,
        (pltpu.VMEM((1024, 4096), F32), shape((128, 512)), shape((8, 640))),
        [VM] * 10,
        "patch_kernel",
    )(rows, cls_protos, *pieces)

    for step in range(ITERS):
        last = step == ITERS - 1
        if step:
            outs = [shape((8, 640))]
            if last:
                outs.append(shape((32, 4, 512)))
            done = call(
                functools.partial(columns_body, last),
                tuple(outs),
                [VM] * 3,
                "column_sums",
                [pltpu.VMEM((8, 4096), F32)],
            )(got, kern, cls_kern)
            message = done[0]
        message = call(add_body, shape((8, 640)), [VM] * 2, "add_core")(message, lax.ppermute(message, BOTH, CORE))
        parts = [lax.ppermute(message, BOTH, swap(dyh=dyh, dyl=dyl)) for dyh, dyl in Y_STEPS]
        send = call(
            functools.partial(rows_body, last),
            shape((32, 24 if last else 16, 128)),
            [VM] * 5,
            "row_sums",
            [pltpu.VMEM((8, 4096), F32)],
        )(message, *parts, kern)
        got = exchange(send, GROUPS_ZX)

    cols, sums = call(settle_body, (shape((32, 1, 512)), shape((8, 128))), [SM, VM], "settle")(where, got)
    cls_scaled = lax.optimization_barrier((done[1], sums))[0]
    cls_scaled = lax.all_to_all(cls_scaled, "dp", 0, 0, tiled=True)
    other = lax.ppermute(sums, BOTH, swap(dyl=1))
    patch_targets = final(where, *gathered, units, cols, sums, other)
    cls_scaled, patch_targets = lax.optimization_barrier((cls_scaled, patch_targets))
    cls_targets = call(cls_final_body, shape((4, 16384), BF16), [SM, VM, VM], "cls_final")(where, cls_scaled, sums)
    return (cls_targets, patch_targets)


def solution(mesh):
    return jax.shard_map(
        per_device,
        mesh=mesh,
        in_specs=(
            P("dp", None),
            P("dp", None, None),
            P("dp", None),
            P(None, ("proto", "dp")),
            P(None, ("proto", "dp")),
        ),
        out_specs=(P("dp", "proto"), P("dp", "proto")),
        check_vma=False,
    )
```

```python
import functools

import jax
import jax.numpy as jnp
import numpy as np
from jax import lax
from jax.experimental import pallas as pl
from jax.experimental.pallas import tpu as pltpu
from jax.sharding import PartitionSpec as P

PROTOS = 131072
ITERS = 3
TEMP = 0.07
SLOPE = float(1.0 / (TEMP * np.log(2.0)))
F32 = jnp.float32
BF16 = jnp.bfloat16
BOTH = ("dp", "proto")
MIB = 1 << 20

NZ, NX = 8, 4


def coords(g):
    d, p = g // 8, g % 8
    return d % 2, (d // 2) % NZ, d // (2 * NZ), p % NX, p // NX


def flat(core, z, yh, x, yl):
    return ((yh * NZ + z) * 2 + core) * 8 + yl * NX + x


def swap(dcore=0, dz=0, dyh=0, dx=0, dyl=0):
    pairs = []
    for g in range(256):
        core, z, yh, x, yl = coords(g)
        pairs.append((g, flat(core ^ dcore, z ^ dz, yh ^ dyh, x ^ dx, yl ^ dyl)))
    return pairs


def groups(key):
    found = {}
    for g in range(256):
        found.setdefault(key(*coords(g)), []).append(g)
    return [found[k] for k in sorted(found)]


CORE = swap(dcore=1)
Y_STEPS = ((1, 1), (1, 0), (0, 1))
GROUPS_Z = groups(lambda core, z, yh, x, yl: (core, yh, x, yl))
GROUPS_ZC = groups(lambda core, z, yh, x, yl: (yh, x, yl))
GROUPS_ZX = groups(lambda core, z, yh, x, yl: (core, yh, yl))


def exchange(value, group):
    return lax.all_to_all(value, BOTH, 0, 0, axis_index_groups=group, tiled=True)


VM = pl.BlockSpec(memory_space=pltpu.VMEM)
SM = pl.BlockSpec(memory_space=pltpu.SMEM)
HBM = pl.BlockSpec(memory_space=pltpu.HBM)


def call(body, out_shape, specs, name, scratch=(), limit=8):
    return pl.pallas_call(
        body,
        out_shape=out_shape,
        in_specs=specs,
        out_specs=jax.tree.map(lambda _: VM, out_shape),
        scratch_shapes=list(scratch),
        compiler_params=pltpu.CompilerParams(vmem_limit_bytes=limit * MIB),
        name=name,
    )


def shape(dims, dtype=F32):
    return jax.ShapeDtypeStruct(dims, dtype)


def down(row):
    return jnp.transpose(jnp.broadcast_to(row, (128, 128)))


def across(block):
    return jnp.sum(jnp.transpose(block), axis=0, keepdims=True)


def summed(got_ref, row):
    total = got_ref[0, row]
    for k in range(1, 32):
        total = total + got_ref[k, row]
    return total


def swapped(rows, step):
    return jnp.concatenate([rows[k ^ step : (k ^ step) + 1] for k in range(8)], axis=0)


def inv_norms(protos):
    wide = protos.astype(F32)
    return SLOPE * lax.rsqrt(jnp.sum(wide * wide, axis=0, keepdims=True) + 1e-06)


def unit(values):
    return (values * lax.rsqrt(jnp.sum(values * values, -1, keepdims=True) + 1e-06)).astype(BF16)


def units_body(feat_ref, mask_ref, unit_ref):
    for image in range(4):
        pick = lax.broadcasted_iota(jnp.int32, (256, 64), 0) == mask_ref[image : image + 1, :]
        chosen = lax.dot_general(
            pick.astype(BF16), feat_ref[image], (((0,), (0,)), ((), ())), preferred_element_type=F32
        )
        unit_ref[image * 64 : image * 64 + 64, :] = unit(chosen)


def send_body(where_ref, unit_ref, cls_ref, a_ref, b_ref, c_ref, send_ref):
    core, yh = where_ref[0], where_ref[2]
    half = unit_ref[pl.ds(pl.multiple_of(where_ref[4] * 128, 128), 128), :]
    cls = [unit(ref[...].astype(F32)).astype(F32) for ref in (cls_ref, a_ref, b_ref, c_ref)]
    near = [jnp.where(core == 0, cls[0], cls[1]), jnp.where(core == 0, cls[1], cls[0])]
    far = [jnp.where(core == 0, cls[2], cls[3]), jnp.where(core == 0, cls[3], cls[2])]
    first = [jnp.where(yh == 0, n, f) for n, f in zip(near, far)]
    second = [jnp.where(yh == 0, f, n) for n, f in zip(near, far)]
    tail = jnp.concatenate(first + second, axis=0).astype(BF16)
    for z in range(NZ):
        send_ref[z, :128, :] = half
        send_ref[z, 128:, :] = tail


def cls_step(cls_kern, row_scale):
    wide = down(row_scale)
    cols = [
        1.0 / jnp.sum(cls_kern[:, q * 128 : q * 128 + 128] * wide, axis=0, keepdims=True)
        for q in range(4)
    ]
    total = cls_kern[:, :128] * cols[0]
    for q in range(1, 4):
        total = total + cls_kern[:, q * 128 : q * 128 + 128] * cols[q]
    return cols, across(total)


def kernel_body(rows_ref, cls_ref, *refs):
    pieces, (kern_ref, cls_kern_ref, message_ref, units_ref, held_ref, sems) = refs[:8], refs[8:]
    copies = [pltpu.make_async_copy(rows_ref, units_ref, sems.at[9])]
    copies += [pltpu.make_async_copy(ref, held_ref.at[k], sems.at[k]) for k, ref in enumerate((*pieces, cls_ref))]
    for copy in copies:
        copy.start()
    copies[0].wait()
    for k in range(8):
        copies[k + 1].wait()
        for half in range(2):
            lanes = slice(half * 256, half * 256 + 256)
            protos = held_ref[k, :, lanes]
            scale = inv_norms(protos)
            total = jnp.zeros((8, 256), F32)
            for part in range(2):
                units = units_ref[part * 4 : part * 4 + 4, :128, :].reshape(512, 384)
                dots = jnp.dot(units, protos, preferred_element_type=F32)
                value = jnp.exp2(dots * scale - SLOPE)
                at = k * 512 + half * 256
                kern_ref[part * 512 : part * 512 + 512, at : at + 256] = value
                total = total + jnp.sum(value.reshape(64, 8, 256), axis=0)
            message_ref[k : k + 1, lanes] = jnp.sum(total, axis=0, keepdims=True)
    copies[9].wait()
    units = jnp.concatenate([units_ref[z, 128:, :] for z in range(NZ)], axis=0)
    protos = held_ref[8]
    dots = jnp.dot(units, protos, preferred_element_type=F32)
    cls_kern_ref[...] = jnp.exp2(dots * inv_norms(protos) - SLOPE)
    _, sums = cls_step(cls_kern_ref[...], jnp.ones((1, 128), F32))
    message_ref[:, 512:] = jnp.broadcast_to(sums, (8, 128))


def columns_body(last, got_ref, kern_ref, cls_kern_ref, message_ref, *more):
    row_scale = [1.0 / summed(got_ref, row) for row in range(9)]
    cls_kern = cls_kern_ref[...]
    cols, sums = cls_step(cls_kern, row_scale[8])
    if last:
        for q in range(4):
            scaled = cls_kern[:, q * 128 : q * 128 + 128] * cols[q]
            for n in range(32):
                z, yh, core = n // 4, (n // 2) % 2, n % 2
                more[0][(yh * NZ + z) * 2 + core, :, q * 128 : q * 128 + 128] = scaled[n * 4 : n * 4 + 4]
    acc = more[-1]
    for z in range(NZ):
        wide = down(row_scale[z]).reshape(16, 8, 128)
        for t in range(32):
            block = kern_ref[z * 128 : z * 128 + 128, t * 128 : t * 128 + 128]
            part = jnp.sum(block.reshape(16, 8, 128) * wide, axis=0)
            if z == 0:
                acc[:, t * 128 : t * 128 + 128] = part
            else:
                acc[:, t * 128 : t * 128 + 128] += part
    for k in range(8):
        message_ref[k : k + 1, :512] = jnp.sum(acc[:, k * 512 : k * 512 + 512], axis=0, keepdims=True)
    message_ref[:, 512:] = jnp.broadcast_to(sums, (8, 128))


def add_body(mine_ref, other_ref, out_ref):
    out_ref[...] = mine_ref[...] + swapped(other_ref[...], 4)


def rows_body(last, mine_ref, a_ref, b_ref, c_ref, kern_ref, send_ref, wide_ref):
    total = mine_ref[...]
    for ref, (dyh, dyl) in zip((a_ref, b_ref, c_ref), Y_STEPS):
        total = total + swapped(ref[...], dyh * 2 + dyl)
    cols = 1.0 / total[:, :512]
    cls = total[:1, 512:]
    for k in range(8):
        wide_ref[:, k * 512 : k * 512 + 512] = jnp.broadcast_to(cols[k : k + 1], (8, 512))
    sums = []
    for z in range(NZ):
        acc = jnp.zeros((16, 8, 128), F32)
        for t in range(32):
            block = kern_ref[z * 128 : z * 128 + 128, t * 128 : t * 128 + 128]
            acc = acc + block.reshape(16, 8, 128) * wide_ref[:, t * 128 : t * 128 + 128][None]
        sums.append(across(acc.reshape(128, 128)))
    own = [cols[k : k + 1, q * 128 : q * 128 + 128] for k in (0, 2, 4, 6) for q in range(4)]
    for k in range(32):
        block = own + [sums[k // NX], cls] if last else sums + [cls]
        for at, row in enumerate(block):
            send_ref[k, at] = row


def settle_body(where_ref, got_ref, cols_ref, sums_ref):
    core, yh, x = where_ref[0], where_ref[2], where_ref[3]
    sums_ref[...] = jnp.concatenate([summed(got_ref, 16), summed(got_ref, 17), jnp.zeros((6, 128), F32)], axis=0)
    for z in range(NZ):
        for cr in range(2):
            for yr in range(2):
                row = (jnp.bitwise_xor(yh, yr) * NZ + z) * 2 + jnp.bitwise_xor(core, cr)
                for q in range(4):
                    at = (cr * 2 + yr) * 4 + q
                    cols_ref[row, :, q * 128 : q * 128 + 128] = got_ref[z * NX + x, at]


def cls_final_body(where_ref, scaled_ref, sums_ref, out_ref):
    base = ((where_ref[1] * 2 + where_ref[2]) * 2 + where_ref[0]) * 4
    scale = PROTOS / sums_ref[1:2, :]
    lane = lax.broadcasted_iota(jnp.int32, (1, 128), 1)
    rows = [jnp.sum(jnp.where(lane == base + v, scale, 0.0), axis=1, keepdims=True) for v in range(4)]
    scale = jnp.concatenate(rows, axis=0)
    for d in range(32):
        out_ref[:, d * 512 : d * 512 + 512] = (scaled_ref[d] * scale).astype(BF16)


PARTS = 8


def final_body(
    where_ref, near_ref, far_ref, units_ref, cols_ref, mine_ref, other_ref, out_ref, wide_ref, in_ref, stage_ref, in_sems, out_sems
):
    yh, yl = where_ref[2], where_ref[4]
    ins, outs, begins = [], [], []
    for n in range(PARTS):
        source = near_ref if n < PARTS // 2 else far_ref
        part = n % (PARTS // 2)
        begin = (yh if n < PARTS // 2 else 1 - yh) * 16 + part * 4
        lanes = pl.ds(pl.multiple_of(begin * 512, 2048), 2048)
        begins.append(begin)
        ins.append(pltpu.make_async_copy(source.at[pl.ds(part * 4, 4)], in_ref.at[n], in_sems.at[n]))
        outs.append(pltpu.make_async_copy(stage_ref.at[n], out_ref.at[:, lanes], out_sems.at[n]))
    for copy in ins:
        copy.start()
    mine, other = mine_ref[:1], other_ref[:1]
    wide_ref[:128] = PROTOS / down(jnp.where(yl == 0, mine, other))
    wide_ref[128:] = PROTOS / down(jnp.where(yl == 0, other, mine))
    for n in range(PARTS):
        ins[n].wait()
        for piece in range(4):
            for at in (0, 256):
                protos = in_ref[n, piece, :, at : at + 256]
                cols = cols_ref[begins[n] + piece][:, at : at + 256]
                dots = jnp.dot(units_ref[...], protos, preferred_element_type=F32)
                value = jnp.exp2(dots * inv_norms(protos) - SLOPE) * cols
                for q in (0, 128):
                    scaled = value[:, q : q + 128] * wide_ref[...]
                    to = piece * 512 + at + q
                    stage_ref[n, :, to : to + 128] = scaled.astype(BF16)
        outs[n].start()
    for copy in outs:
        copy.wait()


def final(where, near, far, units, cols, mine, other):
    return pl.pallas_call(
        final_body,
        out_shape=shape((256, 16384), BF16),
        in_specs=[SM, HBM, HBM, VM, VM, VM, VM],
        out_specs=pl.BlockSpec(memory_space=pl.ANY),
        scratch_shapes=[
            pltpu.VMEM((256, 128), F32),
            pltpu.VMEM((PARTS, 4, 384, 512), BF16),
            pltpu.VMEM((PARTS, 256, 2048), BF16),
            pltpu.SemaphoreType.DMA((PARTS,)),
            pltpu.SemaphoreType.DMA((PARTS,)),
        ],
        compiler_params=pltpu.CompilerParams(vmem_limit_bytes=50 * MIB),
        name="final_scale",
    )(where, near, far, units, cols, mine, other)


def per_device(cls_features, patch_features, mask_index, cls_protos, patch_protos):
    dp, proto = lax.axis_index("dp"), lax.axis_index("proto")
    core, z, yh = dp % 2, (dp // 2) % NZ, dp // (2 * NZ)
    x, yl = proto % NX, proto // NX
    where = jnp.stack([core, z, yh, x, yl]).astype(jnp.int32)

    cls_near = [lax.ppermute(cls_features, BOTH, swap(dcore=c, dyh=h)) for c, h in ((1, 0), (0, 1), (1, 1))]

    near = {(0, 0): patch_protos}
    for dyh, dyl in Y_STEPS:
        near[dyh, dyl] = lax.ppermute(patch_protos, BOTH, swap(dyh=dyh, dyl=dyl))
    pieces = [near[k // 2, k % 2] for k in range(4)]
    pieces += [lax.ppermute(piece, BOTH, CORE) for piece in pieces]

    units = call(units_body, shape((256, 384), BF16), [VM] * 2, "units")(patch_features, mask_index)
    send = call(send_body, shape((NZ, 144, 384), BF16), [SM] + [VM] * 5, "send")(where, units, cls_features, *cls_near)
    rows = exchange(send, GROUPS_Z)

    held = lax.optimization_barrier((patch_protos, near[1, 0], rows, *pieces[1:2], *pieces[3:]))[:2]
    gathered = [lax.all_gather(piece, BOTH, axis_index_groups=GROUPS_ZC) for piece in held]

    kern, cls_kern, message = call(
        kernel_body,
        (pltpu.VMEM((1024, 4096), F32), shape((128, 512)), shape((8, 640))),
        [HBM] * 10,
        "patch_kernel",
        [
            pltpu.VMEM((NZ, 144, 384), BF16),
            pltpu.VMEM((9, 384, 512), BF16),
            pltpu.SemaphoreType.DMA((10,)),
        ],
        limit=43,
    )(rows, cls_protos, *pieces)

    for step in range(ITERS):
        last = step == ITERS - 1
        if step:
            outs = [shape((8, 640))]
            if last:
                outs.append(shape((32, 4, 512)))
            done = call(
                functools.partial(columns_body, last),
                tuple(outs),
                [VM] * 3,
                "column_sums",
                [pltpu.VMEM((8, 4096), F32)],
            )(got, kern, cls_kern)
            message = done[0]
        message = call(add_body, shape((8, 640)), [VM] * 2, "add_core")(message, lax.ppermute(message, BOTH, CORE))
        parts = [lax.ppermute(message, BOTH, swap(dyh=dyh, dyl=dyl)) for dyh, dyl in Y_STEPS]
        send = call(
            functools.partial(rows_body, last),
            shape((32, 18 if last else 9, 1, 128)),
            [VM] * 5,
            "row_sums",
            [pltpu.VMEM((8, 4096), F32)],
        )(message, *parts, kern)
        got = exchange(send, GROUPS_ZX)

    cols, sums = call(settle_body, (shape((32, 1, 512)), shape((8, 128))), [SM, VM], "settle")(where, got)
    cls_scaled = lax.optimization_barrier((done[1], sums))[0]
    cls_scaled = lax.all_to_all(cls_scaled, "dp", 0, 0, tiled=True)
    other = lax.ppermute(sums, BOTH, swap(dyl=1))
    patch_targets = final(where, *gathered, units, cols, sums, other)
    cls_scaled, patch_targets = lax.optimization_barrier((cls_scaled, patch_targets))
    cls_targets = call(cls_final_body, shape((4, 16384), BF16), [SM, VM, VM], "cls_final")(where, cls_scaled, sums)
    return (cls_targets, patch_targets)


def solution(mesh):
    return jax.shard_map(
        per_device,
        mesh=mesh,
        in_specs=(
            P("dp", None),
            P("dp", None, None),
            P("dp", None),
            P(None, ("proto", "dp")),
            P(None, ("proto", "dp")),
        ),
        out_specs=(P("dp", "proto"), P("dp", "proto")),
        check_vma=False,
    )
```

```python
import functools

import jax
import jax.numpy as jnp
import numpy as np
from jax import lax
from jax.experimental import pallas as pl
from jax.experimental.pallas import tpu as pltpu
from jax.sharding import PartitionSpec as P

PROTOS = 131072
ITERS = 3
TEMP = 0.07
SLOPE = float(1.0 / (TEMP * np.log(2.0)))
F32 = jnp.float32
BF16 = jnp.bfloat16
BOTH = ("dp", "proto")
MIB = 1 << 20

NZ, NX = 8, 4


def coords(g):
    d, p = g // 8, g % 8
    return d % 2, (d // 2) % NZ, d // (2 * NZ), p % NX, p // NX


def flat(core, z, yh, x, yl):
    return ((yh * NZ + z) * 2 + core) * 8 + yl * NX + x


def swap(dcore=0, dz=0, dyh=0, dx=0, dyl=0):
    pairs = []
    for g in range(256):
        core, z, yh, x, yl = coords(g)
        pairs.append((g, flat(core ^ dcore, z ^ dz, yh ^ dyh, x ^ dx, yl ^ dyl)))
    return pairs


def groups(key):
    found = {}
    for g in range(256):
        found.setdefault(key(*coords(g)), []).append(g)
    return [found[k] for k in sorted(found)]


CORE = swap(dcore=1)
Y_STEPS = ((1, 1), (1, 0), (0, 1))
GROUPS_Z = groups(lambda core, z, yh, x, yl: (core, yh, x, yl))
GROUPS_ZC = groups(lambda core, z, yh, x, yl: (yh, x, yl))
GROUPS_ZX = groups(lambda core, z, yh, x, yl: (core, yh, yl))


def exchange(value, group):
    return lax.all_to_all(value, BOTH, 0, 0, axis_index_groups=group, tiled=True)


VM = pl.BlockSpec(memory_space=pltpu.VMEM)
SM = pl.BlockSpec(memory_space=pltpu.SMEM)
HBM = pl.BlockSpec(memory_space=pltpu.HBM)


def call(body, out_shape, specs, name, scratch=(), limit=8):
    return pl.pallas_call(
        body,
        out_shape=out_shape,
        in_specs=specs,
        out_specs=jax.tree.map(lambda _: VM, out_shape),
        scratch_shapes=list(scratch),
        compiler_params=pltpu.CompilerParams(vmem_limit_bytes=limit * MIB),
        name=name,
    )


def shape(dims, dtype=F32):
    return jax.ShapeDtypeStruct(dims, dtype)


def down(row):
    return jnp.transpose(jnp.broadcast_to(row, (128, 128)))


def across(block):
    return jnp.sum(jnp.transpose(block), axis=0, keepdims=True)


def summed(got_ref, row):
    total = got_ref[0, row]
    for k in range(1, 32):
        total = total + got_ref[k, row]
    return total


def swapped(rows, step):
    return jnp.concatenate([rows[k ^ step : (k ^ step) + 1] for k in range(8)], axis=0)


def inv_norms(protos):
    wide = protos.astype(F32)
    return SLOPE * lax.rsqrt(jnp.sum(wide * wide, axis=0, keepdims=True) + 1e-06)


def unit(values):
    return (values * lax.rsqrt(jnp.sum(values * values, -1, keepdims=True) + 1e-06)).astype(BF16)


def units_body(feat_ref, mask_ref, unit_ref):
    for image in range(4):
        pick = lax.broadcasted_iota(jnp.int32, (256, 64), 0) == mask_ref[image : image + 1, :]
        chosen = lax.dot_general(
            pick.astype(BF16), feat_ref[image], (((0,), (0,)), ((), ())), preferred_element_type=F32
        )
        unit_ref[image * 64 : image * 64 + 64, :] = unit(chosen)


def send_body(where_ref, unit_ref, cls_ref, a_ref, b_ref, c_ref, send_ref):
    core, yh = where_ref[0], where_ref[2]
    half = unit_ref[pl.ds(pl.multiple_of(where_ref[4] * 128, 128), 128), :]
    cls = [unit(ref[...].astype(F32)).astype(F32) for ref in (cls_ref, a_ref, b_ref, c_ref)]
    near = [jnp.where(core == 0, cls[0], cls[1]), jnp.where(core == 0, cls[1], cls[0])]
    far = [jnp.where(core == 0, cls[2], cls[3]), jnp.where(core == 0, cls[3], cls[2])]
    first = [jnp.where(yh == 0, n, f) for n, f in zip(near, far)]
    second = [jnp.where(yh == 0, f, n) for n, f in zip(near, far)]
    tail = jnp.concatenate(first + second, axis=0).astype(BF16)
    for z in range(NZ):
        send_ref[z, :128, :] = half
        send_ref[z, 128:, :] = tail


def cls_step(cls_kern, row_scale):
    wide = down(row_scale)
    cols = [
        1.0 / jnp.sum(cls_kern[:, q * 128 : q * 128 + 128] * wide, axis=0, keepdims=True)
        for q in range(4)
    ]
    total = cls_kern[:, :128] * cols[0]
    for q in range(1, 4):
        total = total + cls_kern[:, q * 128 : q * 128 + 128] * cols[q]
    return cols, across(total)


def kernel_body(rows_ref, cls_ref, *refs):
    pieces, (kern_ref, cls_kern_ref, message_ref, units_ref, held_ref, sems) = refs[:8], refs[8:]
    copies = [pltpu.make_async_copy(rows_ref, units_ref, sems.at[9])]
    copies += [pltpu.make_async_copy(ref, held_ref.at[k], sems.at[k]) for k, ref in enumerate((*pieces, cls_ref))]
    for copy in copies:
        copy.start()
    copies[0].wait()
    for k in range(8):
        copies[k + 1].wait()
        for half in range(2):
            lanes = slice(half * 256, half * 256 + 256)
            protos = held_ref[k, :, lanes]
            scale = inv_norms(protos)
            total = jnp.zeros((8, 256), F32)
            for part in range(2):
                units = units_ref[part * 4 : part * 4 + 4, :128, :].reshape(512, 384)
                dots = jnp.dot(units, protos, preferred_element_type=F32)
                value = jnp.exp2(dots * scale - SLOPE)
                at = k * 512 + half * 256
                kern_ref[part * 512 : part * 512 + 512, at : at + 256] = value
                total = total + jnp.sum(value.reshape(64, 8, 256), axis=0)
            message_ref[k : k + 1, lanes] = jnp.sum(total, axis=0, keepdims=True)
    copies[9].wait()
    units = jnp.concatenate([units_ref[z, 128:, :] for z in range(NZ)], axis=0)
    protos = held_ref[8]
    dots = jnp.dot(units, protos, preferred_element_type=F32)
    cls_kern_ref[...] = jnp.exp2(dots * inv_norms(protos) - SLOPE)
    _, sums = cls_step(cls_kern_ref[...], jnp.ones((1, 128), F32))
    message_ref[:, 512:] = jnp.broadcast_to(sums, (8, 128))


def columns_body(last, got_ref, kern_ref, cls_kern_ref, message_ref, *more):
    row_scale = [1.0 / summed(got_ref, row) for row in range(9)]
    cls_kern = cls_kern_ref[...]
    cols, sums = cls_step(cls_kern, row_scale[8])
    if last:
        for q in range(4):
            scaled = cls_kern[:, q * 128 : q * 128 + 128] * cols[q]
            for n in range(32):
                z, yh, core = n // 4, (n // 2) % 2, n % 2
                more[0][(yh * NZ + z) * 2 + core, :, q * 128 : q * 128 + 128] = scaled[n * 4 : n * 4 + 4]
    acc = more[-1]
    for z in range(NZ):
        wide = down(row_scale[z]).reshape(16, 8, 128)
        for t in range(32):
            block = kern_ref[z * 128 : z * 128 + 128, t * 128 : t * 128 + 128]
            part = jnp.sum(block.reshape(16, 8, 128) * wide, axis=0)
            if z == 0:
                acc[:, t * 128 : t * 128 + 128] = part
            else:
                acc[:, t * 128 : t * 128 + 128] += part
    for k in range(8):
        message_ref[k : k + 1, :512] = jnp.sum(acc[:, k * 512 : k * 512 + 512], axis=0, keepdims=True)
    message_ref[:, 512:] = jnp.broadcast_to(sums, (8, 128))


def add_body(mine_ref, other_ref, out_ref):
    out_ref[...] = mine_ref[...] + swapped(other_ref[...], 4)


def rows_body(last, mine_ref, a_ref, b_ref, c_ref, kern_ref, send_ref, wide_ref):
    total = mine_ref[...]
    for ref, (dyh, dyl) in zip((a_ref, b_ref, c_ref), Y_STEPS):
        total = total + swapped(ref[...], dyh * 2 + dyl)
    cols = 1.0 / total[:, :512]
    cls = total[:1, 512:]
    for k in range(8):
        wide_ref[:, k * 512 : k * 512 + 512] = jnp.broadcast_to(cols[k : k + 1], (8, 512))
    sums = []
    for z in range(NZ):
        acc = jnp.zeros((16, 8, 128), F32)
        for t in range(32):
            block = kern_ref[z * 128 : z * 128 + 128, t * 128 : t * 128 + 128]
            acc = acc + block.reshape(16, 8, 128) * wide_ref[:, t * 128 : t * 128 + 128][None]
        sums.append(across(acc.reshape(128, 128)))
    own = [cols[k : k + 1, q * 128 : q * 128 + 128] for k in (0, 2, 4, 6) for q in range(4)]
    for k in range(32):
        block = own + [sums[k // NX], cls] if last else sums + [cls]
        for at, row in enumerate(block):
            send_ref[k, at] = row


def settle_body(where_ref, got_ref, cols_ref, sums_ref):
    core, yh, x = where_ref[0], where_ref[2], where_ref[3]
    sums_ref[...] = jnp.concatenate([summed(got_ref, 16), summed(got_ref, 17), jnp.zeros((6, 128), F32)], axis=0)
    for z in range(NZ):
        for cr in range(2):
            for yr in range(2):
                row = (jnp.bitwise_xor(yh, yr) * NZ + z) * 2 + jnp.bitwise_xor(core, cr)
                for q in range(4):
                    at = (cr * 2 + yr) * 4 + q
                    cols_ref[row, :, q * 128 : q * 128 + 128] = got_ref[z * NX + x, at]


def cls_final_body(where_ref, scaled_ref, sums_ref, out_ref):
    base = ((where_ref[1] * 2 + where_ref[2]) * 2 + where_ref[0]) * 4
    scale = PROTOS / sums_ref[1:2, :]
    lane = lax.broadcasted_iota(jnp.int32, (1, 128), 1)
    rows = [jnp.sum(jnp.where(lane == base + v, scale, 0.0), axis=1, keepdims=True) for v in range(4)]
    scale = jnp.concatenate(rows, axis=0)
    for d in range(32):
        out_ref[:, d * 512 : d * 512 + 512] = (scaled_ref[d] * scale).astype(BF16)


PARTS = 8


def final_body(
    where_ref, near_ref, far_ref, units_ref, cols_ref, mine_ref, other_ref, out_ref, wide_ref, in_ref, stage_ref, in_sems, out_sems
):
    yh, yl = where_ref[2], where_ref[4]
    ins, outs, begins = [], [], []
    for n in range(PARTS):
        source = near_ref if n < PARTS // 2 else far_ref
        part = n % (PARTS // 2)
        begin = (yh if n < PARTS // 2 else 1 - yh) * 16 + part * 4
        lanes = pl.ds(pl.multiple_of(begin * 512, 2048), 2048)
        begins.append(begin)
        ins.append(pltpu.make_async_copy(source.at[pl.ds(part * 4, 4)], in_ref.at[n], in_sems.at[n]))
        outs.append(pltpu.make_async_copy(stage_ref.at[n], out_ref.at[:, lanes], out_sems.at[n]))
    for copy in ins:
        copy.start()
    mine, other = mine_ref[:1], other_ref[:1]
    wide_ref[:128] = PROTOS / down(jnp.where(yl == 0, mine, other))
    wide_ref[128:] = PROTOS / down(jnp.where(yl == 0, other, mine))
    for n in range(PARTS):
        ins[n].wait()
        for piece in range(4):
            for at in (0, 256):
                protos = in_ref[n, piece, :, at : at + 256]
                cols = cols_ref[begins[n] + piece][:, at : at + 256]
                dots = jnp.dot(units_ref[...], protos, preferred_element_type=F32)
                value = jnp.exp2(dots * inv_norms(protos) - SLOPE) * cols
                for q in (0, 128):
                    scaled = value[:, q : q + 128] * wide_ref[...]
                    to = piece * 512 + at + q
                    stage_ref[n, :, to : to + 128] = scaled.astype(BF16)
        outs[n].start()
    for copy in outs:
        copy.wait()


def final(where, near, far, units, cols, mine, other):
    return pl.pallas_call(
        final_body,
        out_shape=shape((256, 16384), BF16),
        in_specs=[SM, HBM, HBM, VM, VM, VM, VM],
        out_specs=pl.BlockSpec(memory_space=pl.ANY),
        scratch_shapes=[
            pltpu.VMEM((256, 128), F32),
            pltpu.VMEM((PARTS, 4, 384, 512), BF16),
            pltpu.VMEM((PARTS, 256, 2048), BF16),
            pltpu.SemaphoreType.DMA((PARTS,)),
            pltpu.SemaphoreType.DMA((PARTS,)),
        ],
        compiler_params=pltpu.CompilerParams(vmem_limit_bytes=50 * MIB),
        cost_estimate=pl.CostEstimate(flops=64*256*384*16384, bytes_accessed=512*MIB, transcendentals=1 << 22),
        name="final_scale",
    )(where, near, far, units, cols, mine, other)


def per_device(cls_features, patch_features, mask_index, cls_protos, patch_protos):
    dp, proto = lax.axis_index("dp"), lax.axis_index("proto")
    core, z, yh = dp % 2, (dp // 2) % NZ, dp // (2 * NZ)
    x, yl = proto % NX, proto // NX
    where = jnp.stack([core, z, yh, x, yl]).astype(jnp.int32)

    cls_near = [lax.ppermute(cls_features, BOTH, swap(dcore=c, dyh=h)) for c, h in ((1, 0), (0, 1), (1, 1))]

    near = {(0, 0): patch_protos}
    for dyh, dyl in Y_STEPS:
        near[dyh, dyl] = lax.ppermute(patch_protos, BOTH, swap(dyh=dyh, dyl=dyl))
    pieces = [near[k // 2, k % 2] for k in range(4)]
    pieces += [lax.ppermute(piece, BOTH, CORE) for piece in pieces]

    units = call(units_body, shape((256, 384), BF16), [VM] * 2, "units")(patch_features, mask_index)
    send = call(send_body, shape((NZ, 144, 384), BF16), [SM] + [VM] * 5, "send")(where, units, cls_features, *cls_near)
    rows = exchange(send, GROUPS_Z)

    held = lax.optimization_barrier((patch_protos, near[1, 0], rows, *pieces[1:2], *pieces[3:]))[:2]
    gathered = [lax.all_gather(piece, BOTH, axis_index_groups=GROUPS_ZC) for piece in held]

    kern, cls_kern, message = call(
        kernel_body,
        (pltpu.VMEM((1024, 4096), F32), shape((128, 512)), shape((8, 640))),
        [HBM] * 10,
        "patch_kernel",
        [
            pltpu.VMEM((NZ, 144, 384), BF16),
            pltpu.VMEM((9, 384, 512), BF16),
            pltpu.SemaphoreType.DMA((10,)),
        ],
        limit=43,
    )(rows, cls_protos, *pieces)

    for step in range(ITERS):
        last = step == ITERS - 1
        if step:
            outs = [shape((8, 640))]
            if last:
                outs.append(shape((32, 4, 512)))
            done = call(
                functools.partial(columns_body, last),
                tuple(outs),
                [VM] * 3,
                "column_sums",
                [pltpu.VMEM((8, 4096), F32)],
            )(got, kern, cls_kern)
            message = done[0]
        message = call(add_body, shape((8, 640)), [VM] * 2, "add_core")(message, lax.ppermute(message, BOTH, CORE))
        parts = [lax.ppermute(message, BOTH, swap(dyh=dyh, dyl=dyl)) for dyh, dyl in Y_STEPS]
        send = call(
            functools.partial(rows_body, last),
            shape((32, 18 if last else 9, 1, 128)),
            [VM] * 5,
            "row_sums",
            [pltpu.VMEM((8, 4096), F32)],
        )(message, *parts, kern)
        got = exchange(send, GROUPS_ZX)

    cols, sums = call(settle_body, (shape((32, 1, 512)), shape((8, 128))), [SM, VM], "settle")(where, got)
    cls_scaled = lax.optimization_barrier((done[1], sums))[0]
    cls_scaled = lax.all_to_all(cls_scaled, "dp", 0, 0, tiled=True)
    other = lax.ppermute(sums, BOTH, swap(dyl=1))
    patch_targets = final(where, *gathered, units, cols, sums, other)
    cls_scaled, patch_targets = lax.optimization_barrier((cls_scaled, patch_targets))
    cls_targets = call(cls_final_body, shape((4, 16384), BF16), [SM, VM, VM], "cls_final")(where, cls_scaled, sums)
    return (cls_targets, patch_targets)


def solution(mesh):
    return jax.shard_map(
        per_device,
        mesh=mesh,
        in_specs=(
            P("dp", None),
            P("dp", None, None),
            P("dp", None),
            P(None, ("proto", "dp")),
            P(None, ("proto", "dp")),
        ),
        out_specs=(P("dp", "proto"), P("dp", "proto")),
        check_vma=False,
    )
```

```python
import functools

import jax
import jax.numpy as jnp
import numpy as np
from jax import lax
from jax.experimental import pallas as pl
from jax.experimental.pallas import tpu as pltpu
from jax.sharding import PartitionSpec as P

PROTOS = 131072
ITERS = 3
TEMP = 0.07
SLOPE = float(1.0 / (TEMP * np.log(2.0)))
F32 = jnp.float32
BF16 = jnp.bfloat16
BOTH = ("dp", "proto")
MIB = 1 << 20

NZ, NX = 8, 4


def coords(g):
    d, p = g // 8, g % 8
    return d % 2, (d // 2) % NZ, d // (2 * NZ), p % NX, p // NX


def flat(core, z, yh, x, yl):
    return ((yh * NZ + z) * 2 + core) * 8 + yl * NX + x


def swap(dcore=0, dz=0, dyh=0, dx=0, dyl=0):
    pairs = []
    for g in range(256):
        core, z, yh, x, yl = coords(g)
        pairs.append((g, flat(core ^ dcore, z ^ dz, yh ^ dyh, x ^ dx, yl ^ dyl)))
    return pairs


def groups(key):
    found = {}
    for g in range(256):
        found.setdefault(key(*coords(g)), []).append(g)
    return [found[k] for k in sorted(found)]


CORE = swap(dcore=1)
Y_STEPS = ((1, 1), (1, 0), (0, 1))
GROUPS_Z = groups(lambda core, z, yh, x, yl: (core, yh, x, yl))
GROUPS_ZC = groups(lambda core, z, yh, x, yl: (yh, x, yl))
GROUPS_ZX = groups(lambda core, z, yh, x, yl: (core, yh, yl))


def exchange(value, group):
    return lax.all_to_all(value, BOTH, 0, 0, axis_index_groups=group, tiled=True)


VM = pl.BlockSpec(memory_space=pltpu.VMEM)
SM = pl.BlockSpec(memory_space=pltpu.SMEM)
HBM = pl.BlockSpec(memory_space=pltpu.HBM)


def call(body, out_shape, specs, name, scratch=(), limit=8):
    return pl.pallas_call(
        body,
        out_shape=out_shape,
        in_specs=specs,
        out_specs=jax.tree.map(lambda _: VM, out_shape),
        scratch_shapes=list(scratch),
        compiler_params=pltpu.CompilerParams(vmem_limit_bytes=limit * MIB),
        name=name,
    )


def shape(dims, dtype=F32):
    return jax.ShapeDtypeStruct(dims, dtype)


def down(row):
    return jnp.transpose(jnp.broadcast_to(row, (128, 128)))


def across(block):
    return jnp.sum(jnp.transpose(block), axis=0, keepdims=True)


def summed(got_ref, row):
    total = got_ref[0, row]
    for k in range(1, 32):
        total = total + got_ref[k, row]
    return total


def swapped(rows, step):
    return jnp.concatenate([rows[k ^ step : (k ^ step) + 1] for k in range(8)], axis=0)


def inv_norms(protos):
    wide = protos.astype(F32)
    return SLOPE * lax.rsqrt(jnp.sum(wide * wide, axis=0, keepdims=True) + 1e-06)


def unit(values):
    return (values * lax.rsqrt(jnp.sum(values * values, -1, keepdims=True) + 1e-06)).astype(BF16)


def units_body(feat_ref, mask_ref, unit_ref):
    for image in range(4):
        pick = lax.broadcasted_iota(jnp.int32, (256, 64), 0) == mask_ref[image : image + 1, :]
        chosen = lax.dot_general(
            pick.astype(BF16), feat_ref[image], (((0,), (0,)), ((), ())), preferred_element_type=F32
        )
        unit_ref[image * 64 : image * 64 + 64, :] = unit(chosen)


def send_body(where_ref, unit_ref, cls_ref, a_ref, b_ref, c_ref, send_ref):
    core, yh = where_ref[0], where_ref[2]
    half = unit_ref[pl.ds(pl.multiple_of(where_ref[4] * 128, 128), 128), :]
    cls = [unit(ref[...].astype(F32)).astype(F32) for ref in (cls_ref, a_ref, b_ref, c_ref)]
    near = [jnp.where(core == 0, cls[0], cls[1]), jnp.where(core == 0, cls[1], cls[0])]
    far = [jnp.where(core == 0, cls[2], cls[3]), jnp.where(core == 0, cls[3], cls[2])]
    first = [jnp.where(yh == 0, n, f) for n, f in zip(near, far)]
    second = [jnp.where(yh == 0, f, n) for n, f in zip(near, far)]
    tail = jnp.concatenate(first + second, axis=0).astype(BF16)
    for z in range(NZ):
        send_ref[z, :128, :] = half
        send_ref[z, 128:, :] = tail


def cls_step(cls_kern, row_scale):
    wide = down(row_scale)
    cols = [
        1.0 / jnp.sum(cls_kern[:, q * 128 : q * 128 + 128] * wide, axis=0, keepdims=True)
        for q in range(4)
    ]
    total = cls_kern[:, :128] * cols[0]
    for q in range(1, 4):
        total = total + cls_kern[:, q * 128 : q * 128 + 128] * cols[q]
    return cols, across(total)


def kernel_body(rows_ref, cls_ref, *refs):
    pieces, (kern_ref, cls_kern_ref, message_ref, units_ref, held_ref, sems) = refs[:8], refs[8:]
    copies = [pltpu.make_async_copy(rows_ref, units_ref, sems.at[9])]
    copies += [pltpu.make_async_copy(ref, held_ref.at[k], sems.at[k]) for k, ref in enumerate((*pieces, cls_ref))]
    for copy in copies:
        copy.start()
    copies[0].wait()
    for k in range(8):
        copies[k + 1].wait()
        for half in range(2):
            lanes = slice(half * 256, half * 256 + 256)
            protos = held_ref[k, :, lanes]
            scale = inv_norms(protos)
            total = jnp.zeros((8, 256), F32)
            for part in range(2):
                units = units_ref[part * 4 : part * 4 + 4, :128, :].reshape(512, 384)
                dots = jnp.dot(units, protos, preferred_element_type=F32)
                value = jnp.exp2(dots * scale - SLOPE)
                at = k * 512 + half * 256
                kern_ref[part * 512 : part * 512 + 512, at : at + 256] = value
                total = total + jnp.sum(value.reshape(64, 8, 256), axis=0)
            message_ref[k : k + 1, lanes] = jnp.sum(total, axis=0, keepdims=True)
    copies[9].wait()
    units = jnp.concatenate([units_ref[z, 128:, :] for z in range(NZ)], axis=0)
    protos = held_ref[8]
    dots = jnp.dot(units, protos, preferred_element_type=F32)
    cls_kern_ref[...] = jnp.exp2(dots * inv_norms(protos) - SLOPE)
    _, sums = cls_step(cls_kern_ref[...], jnp.ones((1, 128), F32))
    message_ref[:, 512:] = jnp.broadcast_to(sums, (8, 128))


def columns_body(last, got_ref, kern_ref, cls_kern_ref, message_ref, *more):
    row_scale = [1.0 / summed(got_ref, row) for row in range(9)]
    cls_kern = cls_kern_ref[...]
    cols, sums = cls_step(cls_kern, row_scale[8])
    if last:
        for q in range(4):
            scaled = cls_kern[:, q * 128 : q * 128 + 128] * cols[q]
            for n in range(32):
                z, yh, core = n // 4, (n // 2) % 2, n % 2
                more[0][(yh * NZ + z) * 2 + core, :, q * 128 : q * 128 + 128] = scaled[n * 4 : n * 4 + 4]
    acc = more[-1]
    for z in range(NZ):
        wide = down(row_scale[z]).reshape(16, 8, 128)
        for t in range(32):
            block = kern_ref[z * 128 : z * 128 + 128, t * 128 : t * 128 + 128]
            part = jnp.sum(block.reshape(16, 8, 128) * wide, axis=0)
            if z == 0:
                acc[:, t * 128 : t * 128 + 128] = part
            else:
                acc[:, t * 128 : t * 128 + 128] += part
    for k in range(8):
        message_ref[k : k + 1, :512] = jnp.sum(acc[:, k * 512 : k * 512 + 512], axis=0, keepdims=True)
    message_ref[:, 512:] = jnp.broadcast_to(sums, (8, 128))


def add_body(mine_ref, other_ref, out_ref):
    out_ref[...] = mine_ref[...] + swapped(other_ref[...], 4)


def rows_body(last, mine_ref, a_ref, b_ref, c_ref, kern_ref, send_ref, wide_ref):
    total = mine_ref[...]
    for ref, (dyh, dyl) in zip((a_ref, b_ref, c_ref), Y_STEPS):
        total = total + swapped(ref[...], dyh * 2 + dyl)
    cols = 1.0 / total[:, :512]
    cls = total[:1, 512:]
    for k in range(8):
        wide_ref[:, k * 512 : k * 512 + 512] = jnp.broadcast_to(cols[k : k + 1], (8, 512))
    sums = []
    for z in range(NZ):
        acc = jnp.zeros((16, 8, 128), F32)
        for t in range(32):
            block = kern_ref[z * 128 : z * 128 + 128, t * 128 : t * 128 + 128]
            acc = acc + block.reshape(16, 8, 128) * wide_ref[:, t * 128 : t * 128 + 128][None]
        sums.append(across(acc.reshape(128, 128)))
    own = [cols[k : k + 1, q * 128 : q * 128 + 128] for k in (0, 2, 4, 6) for q in range(4)]
    for k in range(32):
        block = own + [sums[k // NX], cls] if last else sums + [cls]
        for at, row in enumerate(block):
            send_ref[k, at] = row


def settle_body(where_ref, got_ref, cols_ref, sums_ref):
    core, yh, x = where_ref[0], where_ref[2], where_ref[3]
    sums_ref[...] = jnp.concatenate([summed(got_ref, 16), summed(got_ref, 17), jnp.zeros((6, 128), F32)], axis=0)
    for z in range(NZ):
        for cr in range(2):
            for yr in range(2):
                row = (jnp.bitwise_xor(yh, yr) * NZ + z) * 2 + jnp.bitwise_xor(core, cr)
                for q in range(4):
                    at = (cr * 2 + yr) * 4 + q
                    cols_ref[row, :, q * 128 : q * 128 + 128] = got_ref[z * NX + x, at]


def cls_final_body(where_ref, scaled_ref, sums_ref, out_ref):
    base = ((where_ref[1] * 2 + where_ref[2]) * 2 + where_ref[0]) * 4
    scale = PROTOS / sums_ref[1:2, :]
    lane = lax.broadcasted_iota(jnp.int32, (1, 128), 1)
    rows = [jnp.sum(jnp.where(lane == base + v, scale, 0.0), axis=1, keepdims=True) for v in range(4)]
    scale = jnp.concatenate(rows, axis=0)
    for d in range(32):
        out_ref[:, d * 512 : d * 512 + 512] = (scaled_ref[d] * scale).astype(BF16)


PARTS = 8


def final_body(
    where_ref, near_ref, far_ref, units_ref, cols_ref, mine_ref, other_ref, out_ref, wide_ref, in_ref, stage_ref, in_sems, out_sems
):
    yh, yl = where_ref[2], where_ref[4]
    ins, outs, begins = [], [], []
    for n in range(PARTS):
        source = near_ref if n < PARTS // 2 else far_ref
        part = n % (PARTS // 2)
        begin = (yh if n < PARTS // 2 else 1 - yh) * 16 + part * 4
        lanes = pl.ds(pl.multiple_of(begin * 512, 2048), 2048)
        begins.append(begin)
        ins.append(pltpu.make_async_copy(source.at[pl.ds(part * 4, 4)], in_ref.at[n], in_sems.at[n]))
        outs.append(pltpu.make_async_copy(stage_ref.at[n], out_ref.at[:, lanes], out_sems.at[n]))
    for copy in ins:
        copy.start()
    mine, other = mine_ref[:1], other_ref[:1]
    wide_ref[:128] = PROTOS / down(jnp.where(yl == 0, mine, other))
    wide_ref[128:] = PROTOS / down(jnp.where(yl == 0, other, mine))
    for n in range(PARTS):
        ins[n].wait()
        for piece in range(4):
            for at in (0, 256):
                protos = in_ref[n, piece, :, at : at + 256]
                cols = cols_ref[begins[n] + piece][:, at : at + 256]
                dots = jnp.dot(units_ref[...], protos, preferred_element_type=F32)
                value = jnp.exp2(dots * inv_norms(protos) - SLOPE) * cols
                for q in (0, 128):
                    scaled = value[:, q : q + 128] * wide_ref[...]
                    to = piece * 512 + at + q
                    stage_ref[n, :, to : to + 128] = scaled.astype(BF16)
        outs[n].start()
    for copy in outs:
        copy.wait()


def final(where, near, far, units, cols, mine, other):
    return pl.pallas_call(
        final_body,
        out_shape=shape((256, 16384), BF16),
        in_specs=[SM, HBM, HBM, VM, VM, VM, VM],
        out_specs=pl.BlockSpec(memory_space=pl.ANY),
        scratch_shapes=[
            pltpu.VMEM((256, 128), F32),
            pltpu.VMEM((PARTS, 4, 384, 512), BF16),
            pltpu.VMEM((PARTS, 256, 2048), BF16),
            pltpu.SemaphoreType.DMA((PARTS,)),
            pltpu.SemaphoreType.DMA((PARTS,)),
        ],
        compiler_params=pltpu.CompilerParams(vmem_limit_bytes=50 * MIB),
        name="final_scale",
    )(where, near, far, units, cols, mine, other)


def per_device(cls_features, patch_features, mask_index, cls_protos, patch_protos):
    dp, proto = lax.axis_index("dp"), lax.axis_index("proto")
    core, z, yh = dp % 2, (dp // 2) % NZ, dp // (2 * NZ)
    x, yl = proto % NX, proto // NX
    where = jnp.stack([core, z, yh, x, yl]).astype(jnp.int32)

    cls_near = [lax.ppermute(cls_features, BOTH, swap(dcore=c, dyh=h)) for c, h in ((1, 0), (0, 1), (1, 1))]

    near = {(0, 0): patch_protos}
    for dyh, dyl in Y_STEPS:
        near[dyh, dyl] = lax.ppermute(patch_protos, BOTH, swap(dyh=dyh, dyl=dyl))
    pieces = [near[k // 2, k % 2] for k in range(4)]
    pieces += [lax.ppermute(piece, BOTH, CORE) for piece in pieces]

    units = call(units_body, shape((256, 384), BF16), [VM] * 2, "units")(patch_features, mask_index)
    send = call(send_body, shape((NZ, 144, 384), BF16), [SM] + [VM] * 5, "send")(where, units, cls_features, *cls_near)
    rows = exchange(send, GROUPS_Z)

    held = lax.optimization_barrier((patch_protos, near[1, 0], rows, *pieces[1:2], *pieces[3:]))[:2]
    gathered = [lax.all_gather(piece, BOTH, axis_index_groups=GROUPS_ZC) for piece in held]

    kern, cls_kern, message = call(
        kernel_body,
        (pltpu.VMEM((1024, 4096), F32), shape((128, 512)), shape((8, 640))),
        [HBM] * 10,
        "patch_kernel",
        [
            pltpu.VMEM((NZ, 144, 384), BF16),
            pltpu.VMEM((9, 384, 512), BF16),
            pltpu.SemaphoreType.DMA((10,)),
        ],
        limit=43,
    )(rows, cls_protos, *pieces)

    for step in range(ITERS):
        last = step == ITERS - 1
        if step:
            outs = [shape((8, 640))]
            if last:
                outs.append(shape((32, 4, 512)))
            done = call(
                functools.partial(columns_body, last),
                tuple(outs),
                [VM] * 3,
                "column_sums",
                [pltpu.VMEM((8, 4096), F32)],
            )(got, kern, cls_kern)
            message = done[0]
        message = call(add_body, shape((8, 640)), [VM] * 2, "add_core")(message, lax.ppermute(message, BOTH, CORE))
        parts = [lax.ppermute(message, BOTH, swap(dyh=dyh, dyl=dyl)) for dyh, dyl in Y_STEPS]
        send = call(
            functools.partial(rows_body, last),
            shape((32, 18 if last else 9, 1, 128)),
            [VM] * 5,
            "row_sums",
            [pltpu.VMEM((8, 4096), F32)],
        )(message, *parts, kern)
        got = exchange(send, GROUPS_ZX)

    cols, sums = call(settle_body, (shape((32, 1, 512)), shape((8, 128))), [SM, VM], "settle")(where, got)
    cls_scaled = lax.optimization_barrier((done[1], got))[0]
    cls_scaled = lax.all_to_all(cls_scaled, "dp", 0, 0, tiled=True)
    other = lax.ppermute(sums, BOTH, swap(dyl=1))
    patch_targets = final(where, *gathered, units, cols, sums, other)
    cls_scaled, patch_targets = lax.optimization_barrier((cls_scaled, patch_targets))
    cls_targets = call(cls_final_body, shape((4, 16384), BF16), [SM, VM, VM], "cls_final")(where, cls_scaled, sums)
    return (cls_targets, patch_targets)


def solution(mesh):
    return jax.shard_map(
        per_device,
        mesh=mesh,
        in_specs=(
            P("dp", None),
            P("dp", None, None),
            P("dp", None),
            P(None, ("proto", "dp")),
            P(None, ("proto", "dp")),
        ),
        out_specs=(P("dp", "proto"), P("dp", "proto")),
        check_vma=False,
    )
```
